128 devices in a mesh: gx: 16 (over x_hi, z, core), gy: 8 (over x_lo, y).
Axes of the slice: x: 4 (x_hi: 2, x_lo: 2; x = x_hi * 2 + x_lo), y: 4, z: 4, core: 2. Of those that a mesh axis runs over, the one named last changes fastest.
Arguments:
- pressure: bfloat16 [256, 128, 16, 128], P('gx', 'gy'), may hold values from -6 to 6
- cotangent: bfloat16 [256, 128, 16, 128], P('gx', 'gy'), may hold values from -6 to 6
- mix_rows: bfloat16 [128, 128], replicated, may hold values from -0.5 to 0.5
- mix_channels: bfloat16 [16, 16], replicated, may hold values from -1.5 to 1.5
- pointwise: bfloat16 [16, 16], replicated, may hold values from -1.5 to 1.5
Outputs:
- response: bfloat16 [256, 128, 16, 128], P('gx', 'gy')
- grad_pressure: bfloat16 [256, 128, 16, 128], P('gx', 'gy')
- grad_mix_rows: float32 [128, 128], P(None, 'gy')
- grad_mix_channels: float32 [16, 16], replicated
- grad_pointwise: float32 [16, 16], replicated
The draws below stay inside these ranges and needn't reach their ends.
All inputs are finite; a program needn't handle non-finite values.
Results may differ from the reference program's by a relative error of at most 0.001.
Values sent between devices are 32-bit elements; how exact they have to be, the bound alone decides.
No kernel may reach another device: no remote copies, remote signals or barrier semaphores. Data moves between devices by JAX's collectives and lax.ppermute only.
A program may use at most 64 MiB of HBM per device.

```python
import jax
import jax.numpy as jnp
from jax import lax

Y_DEV = 16
CH = 16
DEPTH = 128
LEVELS = 4
NX = 256
NY = 128
N_GY = 8


def block_scale(own_key, extent, split, smallest, largest):
    def one(axis_at, shards_of):
        steps = jax.random.uniform(jax.random.fold_in(jax.random.fold_in(own_key, 6), axis_at), (shards_of,), jnp.float32, smallest / len(split), largest / len(split))
        return jnp.repeat(jnp.exp(steps), extent[axis_at] // shards_of).reshape((-1,) + (1,) * (len(extent) - axis_at - 1))

    loudness = one(*split[0])
    for cut in split[1:]:
        loudness = loudness * one(*cut)
    return loudness


def gaussian(stream_key, shape, deviation, most, shards=(), kind=jnp.bfloat16):
    result = deviation * jax.random.normal(stream_key, shape, jnp.float32)
    if shards:
        result = result * block_scale(stream_key, shape, shards, -0.22, 0.18)
    return jnp.clip(result, -most, most).astype(kind)


def setup_inputs(seed: int = 0) -> dict:
    seeds = jax.random.split(jax.random.key(seed), 6)
    return {
        "pressure": gaussian(seeds[0], (NX, NY, CH, DEPTH), 1.0, 6.0, ((0, 16), (1, 8))),
        "cotangent": gaussian(seeds[1], (NX, NY, CH, DEPTH), 1.0, 6.0, ((0, 16), (1, 8))),
        "mix_rows": gaussian(seeds[2], (NY, NY), NY ** -0.5, 0.5),
        "mix_channels": gaussian(seeds[3], (CH, CH), CH ** -0.5, 1.5),
        "pointwise": gaussian(seeds[4], (CH, CH), CH ** -0.5, 1.5),
    }


HIGH = lax.Precision.HIGHEST

def depth_forward(vectors, width):
    head = vectors[:, :width]
    even = head[:, 0::2]
    odd = head[:, 1::2]
    detail = odd - 0.5 * (even + jnp.roll(even, -1, 1))
    smooth = even + 0.25 * (jnp.roll(detail, 1, 1) + detail)
    return jnp.concatenate([smooth, detail, vectors[:, width:]], 1)

def depth_inverse(vectors, width):
    half = width // 2
    smooth = vectors[:, :half]
    detail = vectors[:, half:width]
    even = smooth - 0.25 * (jnp.roll(detail, 1, 1) + detail)
    odd = detail + 0.5 * (even + jnp.roll(even, -1, 1))
    head = jnp.stack([even, odd], 2).reshape(vectors.shape[0], width)
    return jnp.concatenate([head, vectors[:, width:]], 1)

def lifting_tables(depth, levels):
    identity = jnp.eye(depth, dtype=jnp.float32)
    forward = [depth_forward(identity, depth >> level) for level in range(levels)]
    inverse = [depth_inverse(identity, depth >> level) for level in range(levels)]
    return (forward, inverse)

def along_forward(field):
    even = field[0::2]
    odd = field[1::2]
    detail = odd - 0.5 * (even + jnp.roll(even, -1, 0))
    smooth = even + 0.25 * (jnp.roll(detail, 1, 0) + detail)
    return (smooth, detail)

def along_inverse(smooth, detail):
    even = smooth - 0.25 * (jnp.roll(detail, 1, 0) + detail)
    odd = detail + 0.5 * (even + jnp.roll(even, -1, 0))
    return jnp.stack([even, odd], 1).reshape((2 * even.shape[0],) + even.shape[1:])

def analyse(field, tables):
    details = []
    for level in range(LEVELS):
        smooth, detail = along_forward(field)
        details.append(detail)
        field = jnp.matmul(smooth, tables[level], precision=HIGH)
    return (field, details)

def synthesise(field, details, tables):
    for level in reversed(range(LEVELS)):
        smooth = jnp.matmul(field, tables[level], precision=HIGH)
        field = along_inverse(smooth, details[level])
    return field

def channel_mix(weight, field):
    return jnp.einsum('dc,xycz->xydz', weight, field, precision=HIGH)

def reference(pressure, cotangent, mix_rows, mix_channels, pointwise):
    forward_tables, inverse_tables = lifting_tables(DEPTH, LEVELS)
    rows_w = mix_rows.astype(jnp.float32)
    channel_w = mix_channels.astype(jnp.float32)
    point_w = pointwise.astype(jnp.float32)
    blocks = jnp.arange(N_GY, dtype=jnp.int32)

    def take(array, index):
        return lax.dynamic_slice_in_dim(array, index * Y_DEV, Y_DEV, 1).astype(jnp.float32)

    def join(stacked):
        moved = jnp.moveaxis(stacked, 0, 1)
        return moved.reshape((stacked.shape[1], NY) + stacked.shape[3:])

    def coarse_of(index):
        return analyse(take(pressure, index), forward_tables)[0]
    coarse = join(lax.map(coarse_of, blocks))
    mixed_in = channel_mix(channel_w, coarse)
    mixed = jnp.einsum('ky,xycz->xkcz', rows_w, mixed_in, precision=HIGH)

    def backward_block(index):
        block = take(pressure, index)
        upstream = take(cotangent, index)
        details = analyse(block, forward_tables)[1]
        mixed_block = lax.dynamic_slice_in_dim(mixed, index * Y_DEV, Y_DEV, 1)

        def synth(values, parts):
            return synthesise(values, parts, inverse_tables)
        spectral, synth_back = jax.vjp(synth, mixed_block, details)
        pre = channel_mix(point_w, block) + spectral
        response, gelu_back = jax.vjp(jax.nn.gelu, pre)
        g_pre = gelu_back(upstream)[0]
        g_mixed, g_details = synth_back(g_pre)
        return (block, response, g_pre, g_mixed, g_details)
    g_mixed = join(lax.map(lambda index: backward_block(index)[3], blocks))
    g_mixed_in = jnp.einsum('ky,xkcz->xycz', rows_w, g_mixed, precision=HIGH)
    grad_mix_rows = jnp.einsum('xkcz,xycz->ky', g_mixed, mixed_in, precision=HIGH)
    g_coarse = jnp.einsum('dc,xydz->xycz', channel_w, g_mixed_in, precision=HIGH)
    grad_mix_channels = jnp.einsum('xydz,xycz->dc', g_mixed_in, coarse, precision=HIGH)

    def final_block(index):
        block, response, g_pre, g_unused, g_details = backward_block(index)
        g_coarse_block = lax.dynamic_slice_in_dim(g_coarse, index * Y_DEV, Y_DEV, 1)
        analyse_back = jax.vjp(lambda values: analyse(values, forward_tables), block)[1]
        g_field = analyse_back((g_coarse_block, g_details))[0]
        g_block = jnp.einsum('dc,xydz->xycz', point_w, g_pre, precision=HIGH) + g_field
        partial_point = jnp.einsum('xydz,xycz->dc', g_pre, block, precision=HIGH)
        return (response.astype(jnp.bfloat16), g_block.astype(jnp.bfloat16), partial_point)
    responses, grads, partials = lax.map(final_block, blocks)
    return (join(responses), join(grads), grad_mix_rows, grad_mix_channels, lax.optimization_barrier(jnp.sum(partials, 0)))
```

```python
import jax
import jax.numpy as jnp
import numpy as np
from jax import lax
from jax.sharding import PartitionSpec as P

DEPTH = 128
LEVELS = 4
PLANES = 16
LINES = 16
CH = 16
N_GY = 8
SHIFTS = (-1, 0, 1, 2)

HIGH = lax.Precision.HIGHEST


def lift_rows(rows):
    even, odd = rows[:, 0::2], rows[:, 1::2]
    detail = odd - 0.5 * (even + np.roll(even, -1, 1))
    smooth = even + 0.25 * (np.roll(detail, 1, 1) + detail)
    return smooth, detail


def depth_table():
    table = np.eye(DEPTH)
    for level in range(LEVELS):
        width = DEPTH >> level
        smooth, detail = lift_rows(table[:, :width])
        table = np.concatenate([smooth, detail, table[:, width:]], 1)
    return table


def plane_weights():
    total = 8 * PLANES
    table = np.eye(total)
    for level in range(LEVELS):
        table = lift_rows(table)[0]
    own = table[3 * PLANES : 4 * PLANES]
    return np.stack([own[:, 3 + shift] for shift in SHIFTS])


TABLE = depth_table()
ANALYSE = TABLE.astype(np.float32)
SYNTHESISE = np.linalg.inv(TABLE).astype(np.float32)
WEIGHTS = plane_weights().astype(np.float32)
RISE = (np.arange(PLANES) / PLANES).astype(np.float32)


def moved(block, axis, distance):
    size = lax.axis_size(axis)
    return lax.ppermute(block, axis, [(i, (i + distance) % size) for i in range(size)])


def gathered(block):
    return [block] + [moved(block, "gy", d) for d in range(1, N_GY)]


def shards(pressure, cotangent, mix_rows, mix_channels, pointwise):
    me = lax.axis_index("gy")
    rows_w = mix_rows.astype(jnp.float32)
    channel_w = mix_channels.astype(jnp.float32)
    point_w = pointwise.astype(jnp.float32)
    field = pressure.astype(jnp.float32)
    sources = [lax.rem(me - d + N_GY, N_GY) for d in range(N_GY)]
    own_rows = lax.dynamic_slice_in_dim(rows_w, me * LINES, LINES, 0)
    own_cols = lax.dynamic_slice_in_dim(rows_w, me * LINES, LINES, 1)

    parts = [jnp.einsum("j,jycz->ycz", WEIGHTS[k], field, precision=HIGH) for k in range(4)]
    coarse = parts[1] + moved(parts[0], "gx", -1) + moved(parts[2], "gx", 1) + moved(parts[3], "gx", 2)
    coarse = jnp.matmul(coarse, ANALYSE, precision=HIGH)

    row_mixed = 0.0
    for source, piece in zip(sources, gathered(coarse)):
        weight = lax.dynamic_slice_in_dim(own_rows, source * LINES, LINES, 1)
        row_mixed += jnp.einsum("ky,ycz->kcz", weight, piece, precision=HIGH)
    mixed = jnp.einsum("dc,kcz->kdz", channel_w, row_mixed, precision=HIGH)
    delta = jnp.matmul(mixed - coarse, SYNTHESISE, precision=HIGH)
    after = moved(delta, "gx", -1)

    rise = jnp.asarray(RISE).reshape(PLANES, 1, 1, 1)
    pre = (
        jnp.einsum("dc,xycz->xydz", pointwise, pressure, preferred_element_type=jnp.float32)
        + field
        + delta
        + rise * (after - delta)
    )
    response, gelu_back = jax.vjp(jax.nn.gelu, pre)
    g_pre = gelu_back(cotangent.astype(jnp.float32))[0]

    up = jnp.einsum("j,jycz->ycz", RISE, g_pre, precision=HIGH)
    here = jnp.sum(g_pre, 0) - up
    g_mixed = jnp.matmul(here + moved(up, "gx", 1), SYNTHESISE.T, precision=HIGH)
    part_channels = jnp.einsum("kdz,kcz->dc", g_mixed, row_mixed, precision=HIGH)
    part_point = jnp.einsum("xydz,xycz->dc", g_pre, field, precision=HIGH)
    g_chan = jnp.einsum("dc,kdz->kcz", channel_w, g_mixed, precision=HIGH)
    small = jnp.stack([part_channels, part_point]).reshape(4, 128)
    pieces = gathered(jnp.concatenate([g_chan.reshape(256, 128), small], 0))
    small = sum(piece[256:] for piece in pieces)
    g_coarse = 0.0
    part_rows = []
    for source, piece in zip(sources, pieces):
        plane = piece[:256].reshape(16, 16, 128)
        weight = lax.dynamic_slice_in_dim(own_cols, source * LINES, LINES, 0)
        g_coarse += jnp.einsum("ky,kcz->ycz", weight, plane, precision=HIGH)
        part_rows.append(jnp.einsum("kcz,ycz->ky", plane, coarse, precision=HIGH))
    spread = jnp.matmul(g_coarse - g_mixed, ANALYSE.T, precision=HIGH)
    around = [moved(spread, "gx", 1), spread, moved(spread, "gx", -1), moved(spread, "gx", -2)]
    g_field = sum(
        jnp.asarray(WEIGHTS[k]).reshape(PLANES, 1, 1, 1) * around[k] for k in range(4)
    )
    grad_pressure = jnp.einsum("dc,xydz->xycz", point_w, g_pre, precision=HIGH) + g_pre + g_field

    place = jnp.zeros((128, 16), jnp.float32)
    for source, block in zip(sources, part_rows):
        place = lax.dynamic_update_slice_in_dim(place, block, source * LINES, 0)
    flat = jnp.concatenate([place.reshape(16, 128), small], 0)
    flat = jnp.broadcast_to(flat[None], (16, 20, 128))
    total = jnp.sum(lax.all_to_all(flat, "gx", 0, 0), 0)
    grad_rows = total[:16].reshape(128, 16)
    grad_channels = total[16:18].reshape(16, 16)
    grad_point = total[18:].reshape(16, 16)
    return (
        response.astype(jnp.bfloat16),
        grad_pressure.astype(jnp.bfloat16),
        grad_rows,
        grad_channels,
        grad_point,
    )


def solution(mesh):
    return jax.shard_map(
        shards,
        mesh=mesh,
        in_specs=(P("gx", "gy", None, None), P("gx", "gy", None, None), P(), P(), P()),
        out_specs=(P("gx", "gy", None, None), P("gx", "gy", None, None), P(None, "gy"), P(), P()),
        check_vma=False,
    )
```

```python
import jax
import jax.numpy as jnp
import numpy as np
from jax import lax
from jax.sharding import PartitionSpec as P

DEPTH = 128
LEVELS = 4
PLANES = 16
LINES = 16
CH = 16
N_GY = 8
RING = 4
SHIFTS = (-1, 0, 1, 2)

HIGH = lax.Precision.HIGHEST


def lift_rows(rows):
    even, odd = rows[:, 0::2], rows[:, 1::2]
    detail = odd - 0.5 * (even + np.roll(even, -1, 1))
    smooth = even + 0.25 * (np.roll(detail, 1, 1) + detail)
    return smooth, detail


def depth_table():
    table = np.eye(DEPTH)
    for level in range(LEVELS):
        width = DEPTH >> level
        smooth, detail = lift_rows(table[:, :width])
        table = np.concatenate([smooth, detail, table[:, width:]], 1)
    return table


def plane_weights():
    total = 8 * PLANES
    table = np.eye(total)
    for level in range(LEVELS):
        table = lift_rows(table)[0]
    own = table[3 * PLANES : 4 * PLANES]
    return np.stack([own[:, 3 + shift] for shift in SHIFTS])


TABLE = depth_table()
ANALYSE = TABLE.astype(np.float32)
SYNTHESISE = np.linalg.inv(TABLE).astype(np.float32)
WEIGHTS = plane_weights().astype(np.float32)
RISE = (np.arange(PLANES) / PLANES).astype(np.float32)


def moved(block, distance):
    size = lax.axis_size("gx")
    return lax.ppermute(block, "gx", [(i, (i + distance) % size) for i in range(size)])


def across(block):
    return lax.ppermute(block, "gy", [(i, (i + RING) % N_GY) for i in range(N_GY)])


def along(block, distance):
    route = [(i, i // RING * RING + (i + distance) % RING) for i in range(N_GY)]
    return lax.ppermute(block, "gy", route)


def shards(pressure, cotangent, mix_rows, mix_channels, pointwise):
    me = lax.axis_index("gy")
    side, spot = me // RING, lax.rem(me, RING)
    rows_w = mix_rows.astype(jnp.float32)
    channel_w = mix_channels.astype(jnp.float32)
    point_w = pointwise.astype(jnp.float32)
    field = pressure.astype(jnp.float32)

    def block(k_side, k_spot, y_side, y_spot):
        k_at = (k_side * RING + lax.rem(k_spot + RING, RING)) * LINES
        y_at = (y_side * RING + lax.rem(y_spot + RING, RING)) * LINES
        return lax.dynamic_slice(rows_w, (k_at, y_at), (LINES, LINES))

    parts = [jnp.einsum("j,jycz->ycz", WEIGHTS[k], field, precision=HIGH) for k in range(4)]
    coarse = parts[1] + moved(parts[3], 2) + moved(parts[0], -1) + moved(parts[2], 1)
    coarse = jnp.matmul(coarse, ANALYSE, precision=HIGH)
    other = across(coarse)

    def partial_mix(distance):
        own = jnp.einsum("ky,ycz->kcz", block(side, spot + distance, side, spot), coarse, precision=HIGH)
        far = block(side, spot + distance, 1 - side, spot)
        return own + jnp.einsum("ky,ycz->kcz", far, other, precision=HIGH)

    sent = [along(partial_mix(d), d) for d in (2, 1, 3)]
    row_mixed = partial_mix(0) + sent[0] + sent[1] + sent[2]
    mixed = jnp.einsum("dc,kcz->kdz", channel_w, row_mixed, precision=HIGH)
    delta = jnp.matmul(mixed - coarse, SYNTHESISE, precision=HIGH)
    after = moved(delta, -1)

    rise = jnp.asarray(RISE).reshape(PLANES, 1, 1, 1)
    pre = (
        jnp.einsum("dc,xycz->xydz", pointwise, pressure, preferred_element_type=jnp.float32)
        + field
        + delta
        + rise * (after - delta)
    )
    response, gelu_back = jax.vjp(jax.nn.gelu, pre)
    g_pre = gelu_back(cotangent.astype(jnp.float32))[0]

    up = jnp.einsum("j,jycz->ycz", RISE, g_pre, precision=HIGH)
    here = jnp.sum(g_pre, 0) - up
    g_mixed = jnp.matmul(here + moved(up, 1), SYNTHESISE.T, precision=HIGH)
    part_channels = jnp.einsum("kdz,kcz->dc", g_mixed, row_mixed, precision=HIGH)
    part_point = jnp.einsum("xydz,xycz->dc", g_pre, field, precision=HIGH)
    g_chan = jnp.einsum("dc,kdz->kcz", channel_w, g_mixed, precision=HIGH)
    small = jnp.stack([part_channels, part_point]).reshape(4, 128)
    small = jnp.concatenate([small, jnp.zeros((4, 128), jnp.float32)], 0)
    packed = jnp.concatenate([g_chan.reshape(256, 128), small], 0)
    pieces = [packed] + [along(packed, d) for d in (2, 1, 3)]
    small = pieces[0][256:260] + pieces[1][256:260] + pieces[2][256:260] + pieces[3][256:260]
    planes = [piece[:256].reshape(16, 16, 128) for piece in pieces]
    back = (0, 2, 1, 3)

    def partial_lines(y_side):
        return sum(
            jnp.einsum("ky,kcz->ycz", block(side, spot - d, y_side, spot), plane, precision=HIGH)
            for d, plane in zip(back, planes)
        )

    def row_grads(lines):
        grads = [jnp.einsum("kcz,ycz->ky", plane, lines, precision=HIGH) for plane in planes]
        return jnp.concatenate(grads, 0)

    far = jnp.concatenate(
        [
            partial_lines(1 - side).reshape(256, 128),
            row_grads(other).reshape(8, 128),
            small,
            jnp.zeros((4, 128), jnp.float32),
        ],
        0,
    )
    far = across(far)
    g_coarse = partial_lines(side) + far[:256].reshape(16, 16, 128)
    spread = jnp.matmul(g_coarse - g_mixed, ANALYSE.T, precision=HIGH)
    around = [None, spread, None, None]
    around[3] = moved(spread, -2)
    around[0] = moved(spread, 1)
    around[2] = moved(spread, -1)
    g_field = sum(
        jnp.asarray(WEIGHTS[k]).reshape(PLANES, 1, 1, 1) * around[k] for k in range(4)
    )
    grad_pressure = jnp.einsum("dc,xydz->xycz", point_w, g_pre, precision=HIGH) + g_pre + g_field

    place = jnp.zeros((128, 16), jnp.float32)
    for k_side, grads in ((side, row_grads(coarse)), (1 - side, far[256:264].reshape(64, 16))):
        for n, d in enumerate(back):
            at = (k_side * RING + lax.rem(spot - d + RING, RING)) * LINES
            place = lax.dynamic_update_slice_in_dim(place, grads[n * 16 : n * 16 + 16], at, 0)
    flat = jnp.concatenate([place.reshape(16, 128), small + far[264:268]], 0)
    flat = jnp.broadcast_to(flat[None], (16, 20, 128))
    total = jnp.sum(lax.all_to_all(flat, "gx", 0, 0), 0)
    grad_rows = total[:16].reshape(128, 16)
    grad_channels = total[16:18].reshape(16, 16)
    grad_point = total[18:].reshape(16, 16)
    return (
        response.astype(jnp.bfloat16),
        grad_pressure.astype(jnp.bfloat16),
        grad_rows,
        grad_channels,
        grad_point,
    )


def solution(mesh):
    return jax.shard_map(
        shards,
        mesh=mesh,
        in_specs=(P("gx", "gy", None, None), P("gx", "gy", None, None), P(), P(), P()),
        out_specs=(P("gx", "gy", None, None), P("gx", "gy", None, None), P(None, "gy"), P(), P()),
        check_vma=False,
    )
```

```python
import jax
import jax.numpy as jnp
import numpy as np
from jax import lax
from jax.experimental import pallas as pl
from jax.experimental.pallas import tpu as pltpu
from jax.sharding import PartitionSpec as P

DEPTH = 128
LEVELS = 4
PLANES = 16
LINES = 16
CH = 16
N_GY = 8
RING = 4
ROWS = 64
LIMIT = 12
GELU_A = float(np.sqrt(2.0 / np.pi))
GELU_B = 0.044715 * GELU_A
SHIFTS = (-1, 0, 1, 2)

HIGH = lax.Precision.HIGHEST


def lift_rows(rows):
    even, odd = rows[:, 0::2], rows[:, 1::2]
    detail = odd - 0.5 * (even + np.roll(even, -1, 1))
    smooth = even + 0.25 * (np.roll(detail, 1, 1) + detail)
    return smooth, detail


def depth_table():
    table = np.eye(DEPTH)
    for level in range(LEVELS):
        width = DEPTH >> level
        smooth, detail = lift_rows(table[:, :width])
        table = np.concatenate([smooth, detail, table[:, width:]], 1)
    return table


def plane_weights():
    total = 8 * PLANES
    table = np.eye(total)
    for level in range(LEVELS):
        table = lift_rows(table)[0]
    own = table[3 * PLANES : 4 * PLANES]
    return np.stack([own[:, 3 + shift] for shift in SHIFTS])


TABLE = depth_table()
ANALYSE = TABLE.astype(np.float32)
SYNTHESISE = np.linalg.inv(TABLE).astype(np.float32)
WEIGHTS = plane_weights().astype(np.float32)
RISE = (np.arange(PLANES) / PLANES).astype(np.float32)


def moved(block, distance):
    size = lax.axis_size("gx")
    return lax.ppermute(block, "gx", [(i, (i + distance) % size) for i in range(size)])


def routed(block, *hops):
    size = lax.axis_size("gx")
    route = [(i, (i + hops[i % 2]) % size) for i in range(size)]
    return lax.ppermute(block, "gx", route)


def across(block):
    return lax.ppermute(block, "gy", [(i, (i + RING) % N_GY) for i in range(N_GY)])


def along(block, distance):
    route = [(i, i // RING * RING + (i + distance) % RING) for i in range(N_GY)]
    return lax.ppermute(block, "gy", route)


def plane_sums(field_ref, own_ref, inner_ref, outer_ref, even_ref, odd_ref):
    odd = lax.rem(lax.axis_index("gx"), 2) == 1
    for first in range(0, LINES * CH, 32):
        rows = pl.ds(first, 32)
        sums = [None] * 4
        for j in range(PLANES):
            plane = field_ref[j, rows, :].astype(jnp.float32)
            for k in range(4):
                if WEIGHTS[k, j] != 0.0:
                    term = plane * float(WEIGHTS[k, j])
                    sums[k] = term if sums[k] is None else sums[k] + term
        own_ref[rows, :] = sums[1]
        inner_ref[rows, :] = jnp.where(odd, sums[0], sums[2])
        outer_ref[rows, :] = jnp.where(odd, sums[2], sums[0])
        even_ref[rows, :] = jnp.where(odd, 0.0, sums[3])
        odd_ref[rows, :] = jnp.where(odd, sums[3], 0.0)


def prepare(table_ref, point_ref, after_ref, kept_ref, map_ref, turned_ref):
    kept_ref[...] = table_ref[...]
    at_row = lax.broadcasted_iota(jnp.int32, (ROWS, CH), 0)
    at_column = lax.broadcasted_iota(jnp.int32, (ROWS, CH), 1)
    tall = (lax.rem(at_row, CH) == at_column).astype(jnp.bfloat16)
    at_row = lax.broadcasted_iota(jnp.int32, (ROWS, ROWS), 0)
    at_column = lax.broadcasted_iota(jnp.int32, (ROWS, ROWS), 1)
    same = at_row // CH == at_column // CH
    point = point_ref[...]
    for turn, dims in enumerate(((1, 0), (1, 1))):
        mapped = lax.dot_general(
            tall, point, (((dims[0],), (dims[1],)), ((), ())), preferred_element_type=jnp.float32
        )
        mapped = lax.dot_general(
            mapped.astype(jnp.bfloat16), tall, (((1,), (1,)), ((), ())), preferred_element_type=jnp.float32
        )
        mapped = jnp.where(same, mapped, 0.0).astype(jnp.bfloat16)
        if turn:
            turned_ref[...] = jnp.concatenate([mapped, mapped], 1)
        else:
            map_ref[...] = mapped


def combine(table_ref, *refs):
    total = sum(ref[...] for ref in refs[:-1])
    refs[-1][...] = jnp.dot(total, table_ref[...], precision=HIGH, preferred_element_type=jnp.float32)


def point_map(point_ref, field_ref, cotangent_ref, out_ref, field_kept_ref, cotangent_kept_ref):
    point = point_ref[...]

    @pl.loop(0, STEPS)
    def _(step):
        rows = pl.ds(pl.multiple_of(step * ROWS, ROWS), ROWS)
        for j in range(0, PLANES, 2):
            pair = jnp.concatenate([field_ref[j, rows, :], field_ref[j + 1, rows, :]], 1)
            mapped = jnp.dot(point, pair, preferred_element_type=jnp.float32) + pair.astype(jnp.float32)
            for n in range(2):
                out_ref[j + n, rows, :] = mapped[:, n * DEPTH : n * DEPTH + DEPTH]
                field_kept_ref[j + n, rows, :] = field_ref[j + n, rows, :]
                cotangent_kept_ref[j + n, rows, :] = cotangent_ref[j + n, rows, :]


def activate(
    turned_ref, mapped_ref, field_ref, cotangent_ref, delta_ref, after_ref,
    response_ref, base_ref, here_ref, up_ref, grad_ref, kept_ref, g_ref, acc_ref, sems,
):
    def chunk(step):
        rows = pl.ds(step * ROWS, ROWS)
        return pltpu.make_async_copy(kept_ref.at[:, rows, :], response_ref.at[:, rows, :], sems.at[step])

    turned = turned_ref[...]
    acc_ref[...] = jnp.zeros_like(acc_ref)
    for step in range(STEPS):
        for first in range(0, ROWS, 32):
            rows = pl.ds(step * ROWS + first, 32)
            delta = delta_ref[rows, :]
            slope = (after_ref[rows, :] - delta) * (1.0 / PLANES)
            base = delta + slope * float(PLANES)
            total = jnp.zeros_like(delta)
            up = jnp.zeros_like(delta)
            for at in range(PLANES - 1, -1, -1):
                base = base - slope
                value = mapped_ref[at, rows, :] + base
                square = value * value
                half = 0.5 + 0.5 * jnp.tanh(value * (GELU_A + GELU_B * square))
                active = value * half
                kept_ref[at, rows, :] = active.astype(jnp.bfloat16)
                rate = half + (active * (1.0 - half)) * (2.0 * GELU_A + 6.0 * GELU_B * square)
                g_pre = rate * cotangent_ref[at, rows, :].astype(jnp.float32)
                g_ref[at, pl.ds(first, 32), :] = g_pre
                total = total + g_pre
                if at:
                    up = up + total
            up = up * (1.0 / PLANES)
            here_ref[rows, :] = total - up
            up_ref[rows, :] = up
        chunk(step).start()
        rows = pl.ds(step * ROWS, ROWS)
        acc = acc_ref[...]
        for j in range(PLANES):
            g_pre = g_ref[j]
            high = g_pre.astype(jnp.bfloat16)
            low = (g_pre - high.astype(jnp.float32)).astype(jnp.bfloat16)
            base_ref[j, rows, :] = g_pre + jnp.dot(
                turned, jnp.concatenate([high, low], 0), preferred_element_type=jnp.float32
            )
            plane = field_ref[j, rows, :]
            acc = acc + lax.dot_general(
                jnp.concatenate([high, low], 1),
                jnp.concatenate([plane, plane], 1),
                (((1,), (1,)), ((), ())),
                preferred_element_type=jnp.float32,
            )
        acc_ref[...] = acc

    row = lax.broadcasted_iota(jnp.int32, (ROWS, ROWS), 0)
    column = lax.broadcasted_iota(jnp.int32, (ROWS, ROWS), 1)
    kept = jnp.where(row // CH == column // CH, acc_ref[...], 0.0)
    folded = kept[0:CH]
    for n in range(1, ROWS // CH):
        folded = folded + kept[n * CH : n * CH + CH]
    source = lax.broadcasted_iota(jnp.int32, (ROWS, DEPTH), 0)
    target = lax.broadcasted_iota(jnp.int32, (ROWS, DEPTH), 1)
    fold = (lax.rem(source, CH) + CH == target).astype(jnp.float32)
    grad_ref[...] = jnp.dot(folded, fold, precision=HIGH, preferred_element_type=jnp.float32)
    for step in range(STEPS):
        chunk(step).wait()


def row_products(own_ref, other_ref, after_ref, *refs):
    out_ref, pieces = refs[-1], refs[:-1]
    total = jnp.zeros((2 * LINES, RING * LINES), jnp.float32)
    for c in range(CH):
        lines = pl.ds(c, LINES, stride=CH)
        left = jnp.concatenate([own_ref[lines, :], other_ref[lines, :]], 0)
        right = jnp.concatenate([ref[lines, :] for ref in pieces], 0)
        total = total + lax.dot_general(
            left, right, (((1,), (1,)), ((), ())), precision=HIGH, preferred_element_type=jnp.float32
        )
    small = pl.ds(LINES * CH, CH)
    products = jnp.concatenate([total[:LINES], total[LINES:]], 1)
    sums = sum(ref[small, :] for ref in pieces)
    for n in range(PLANES):
        out_ref[n, 0:LINES, :] = products
        out_ref[n, LINES:, :] = sums


def spread_out(base_ref, own_ref, inner_ref, outer_ref, even_ref, odd_ref, out_ref, kept_ref, sems):
    odd = lax.rem(lax.axis_index("gx"), 2) == 1

    def chunk(step):
        rows = pl.ds(step * ROWS, ROWS)
        return pltpu.make_async_copy(kept_ref.at[:, rows, :], out_ref.at[:, rows, :], sems.at[step])

    for step in range(STEPS):
        for first in range(step * ROWS, (step + 1) * ROWS, 32):
            rows = pl.ds(first, 32)
            inner, outer = inner_ref[rows, :], outer_ref[rows, :]
            around = [
                jnp.where(odd, inner, outer),
                own_ref[rows, :],
                jnp.where(odd, outer, inner),
                jnp.where(odd, odd_ref[rows, :], even_ref[rows, :]),
            ]
            for j in range(PLANES):
                total = base_ref[j, rows, :]
                for k in range(4):
                    if WEIGHTS[k, j] != 0.0:
                        total = total + around[k] * float(WEIGHTS[k, j])
                kept_ref[j, rows, :] = total.astype(jnp.bfloat16)
        chunk(step).start()
    for step in range(STEPS):
        chunk(step).wait()


STEPS = LINES * CH // ROWS


def plane_of(kind):
    return jax.ShapeDtypeStruct((LINES * CH, DEPTH), kind)


def stack_of(kind):
    return jax.ShapeDtypeStruct((PLANES, LINES * CH, DEPTH), kind)


def add_up(parts_ref, out_ref):
    total = parts_ref[0]
    for n in range(1, PLANES):
        total = total + parts_ref[n]
    out_ref[...] = total


def finish(own_ref, their_ref, placed_ref, rows_ref, channels_ref, point_ref):
    joined = jnp.concatenate([own_ref[0:LINES, 0:64], their_ref[0:LINES, 64:128]], 1)
    rows_ref[...] = jnp.dot(joined, placed_ref[...], precision=HIGH, preferred_element_type=jnp.float32)
    small = own_ref[LINES:, :] + their_ref[LINES:, :]
    channels_ref[...] = small[:, 0:CH]
    point_ref[...] = small[:, CH : 2 * CH]


VMEM = pl.BlockSpec()
HBM = pl.BlockSpec(memory_space=pltpu.HBM)
ANY = pl.BlockSpec(memory_space=pl.ANY)
SENT = [pltpu.VMEM((PLANES, LINES * CH, DEPTH), jnp.bfloat16), pltpu.SemaphoreType.DMA((STEPS,))]


def run(kernel, out_shape, flops, size, scratch=(), **where):
    return pl.pallas_call(
        kernel,
        out_shape=out_shape,
        scratch_shapes=scratch,
        cost_estimate=pl.CostEstimate(flops=flops, bytes_accessed=size, transcendentals=0),
        compiler_params=pltpu.CompilerParams(vmem_limit_bytes=LIMIT * 1024 * 1024),
        **where,
    )


def shards(pressure, cotangent, mix_rows, mix_channels, pointwise):
    me = lax.axis_index("gy")
    side, spot = me // RING, lax.rem(me, RING)
    rows_w = mix_rows.astype(jnp.float32)
    channel_w = mix_channels.astype(jnp.float32)
    field = pressure.reshape(PLANES, LINES * CH, DEPTH)
    upstream = cotangent.reshape(PLANES, LINES * CH, DEPTH)

    def block(k_side, k_spot, y_side, y_spot):
        k_at = (k_side * RING + lax.rem(k_spot + RING, RING)) * LINES
        y_at = (y_side * RING + lax.rem(y_spot + RING, RING)) * LINES
        return lax.dynamic_slice(rows_w, (k_at, y_at), (LINES, LINES))

    own, inner, outer, even, odd = run(plane_sums, [plane_of(jnp.float32)] * 5, 1 << 22, 3 << 19)(field)
    table, point, turned = run(
        prepare,
        [
            jax.ShapeDtypeStruct((DEPTH, DEPTH), jnp.float32),
            jax.ShapeDtypeStruct((ROWS, ROWS), jnp.bfloat16),
            jax.ShapeDtypeStruct((ROWS, 2 * ROWS), jnp.bfloat16),
        ],
        1 << 20,
        1 << 18,
        in_specs=[VMEM, VMEM, ANY],
    )(jnp.asarray(ANALYSE), pointwise, own)
    coarse = run(combine, plane_of(jnp.float32), 1 << 23, 1 << 19)(
        table, own, routed(inner, 1, -1), routed(outer + routed(even, 1, -1), -1, 1), routed(odd, 0, 2)
    ).reshape(LINES, CH, DEPTH)
    point_values, field, upstream = run(
        point_map,
        [stack_of(jnp.float32), stack_of(jnp.bfloat16), stack_of(jnp.bfloat16)],
        1 << 26,
        7 << 20,
    )(point, field, upstream)
    other = across(coarse)

    def partial_mix(distance):
        own = jnp.einsum("ky,ycz->kcz", block(side, spot + distance, side, spot), coarse, precision=HIGH)
        far = block(side, spot + distance, 1 - side, spot)
        return own + jnp.einsum("ky,ycz->kcz", far, other, precision=HIGH)

    sent = [along(partial_mix(d), d) for d in (2, 1, 3)]
    row_mixed = partial_mix(0) + sent[0] + sent[1] + sent[2]
    mixed = jnp.einsum("dc,kcz->kdz", channel_w, row_mixed, precision=HIGH)
    delta = jnp.matmul(mixed - coarse, SYNTHESISE, precision=HIGH)
    after = moved(delta, -1)

    response, base, here, up, part_point = run(
        activate,
        [
            stack_of(jnp.bfloat16),
            stack_of(jnp.float32),
            plane_of(jnp.float32),
            plane_of(jnp.float32),
            jax.ShapeDtypeStruct((CH, DEPTH), jnp.float32),
        ],
        1 << 28,
        5 << 20,
        [
            SENT[0],
            pltpu.VMEM((PLANES, ROWS, DEPTH), jnp.float32),
            pltpu.VMEM((ROWS, ROWS), jnp.float32),
            SENT[1],
        ],
        in_specs=[VMEM] * 6,
        out_specs=[HBM, VMEM, VMEM, VMEM, VMEM],
    )(turned, point_values, field, upstream, delta.reshape(-1, DEPTH), after.reshape(-1, DEPTH))

    below = moved(up, 1)
    g_mixed = jnp.matmul((here + below).reshape(LINES, CH, DEPTH), SYNTHESISE.T, precision=HIGH)
    part_channels = jnp.einsum("kdz,kcz->dc", g_mixed, row_mixed, precision=HIGH)
    g_chan = jnp.einsum("dc,kdz->kcz", channel_w, g_mixed, precision=HIGH)
    small = part_point + jnp.pad(part_channels, ((0, 0), (0, DEPTH - CH)))
    packed = jnp.concatenate([g_chan.reshape(256, 128), small], 0)
    pieces = [packed] + [along(packed, d) for d in (2, 1, 3)]
    planes = [piece[:256].reshape(16, 16, 128) for piece in pieces]
    back = (0, 2, 1, 3)

    def partial_lines(y_side):
        return sum(
            jnp.einsum("ky,kcz->ycz", block(side, spot - d, y_side, spot), plane, precision=HIGH)
            for d, plane in zip(back, planes)
        )

    for_them = partial_lines(1 - side)
    far = across(for_them)
    products = run(
        row_products,
        jax.ShapeDtypeStruct((PLANES, 32, 128), jnp.float32),
        1 << 25,
        1 << 20,
        in_specs=[VMEM, VMEM, ANY] + [VMEM] * RING,
    )(coarse.reshape(256, 128), other.reshape(256, 128), for_them, *pieces)
    products = run(add_up, jax.ShapeDtypeStruct((32, 128), jnp.float32), 1 << 16, 1 << 18)(
        lax.all_to_all(products, "gx", 0, 0)
    )
    their_products = across(products)
    g_coarse = partial_lines(side) + far
    spread = jnp.matmul(g_coarse - g_mixed, ANALYSE.T, precision=HIGH).reshape(256, 128)
    outer = routed(spread, -1, 1)
    around = [spread, routed(spread, 1, -1), outer, routed(outer, 1, -1), routed(spread, 0, -2)]
    at = lax.broadcasted_iota(jnp.int32, (128, 128), 0)
    turn = jnp.asarray(np.repeat(np.array(back * 2), 16))[:, None]
    k_side = jnp.where(at < 64, side, 1 - side)
    k_at = (k_side * RING + lax.rem(spot - turn + RING, RING)) * LINES + lax.rem(at, LINES)
    placed = (k_at == lax.broadcasted_iota(jnp.int32, (128, 128), 1)).astype(jnp.float32)
    grad_pressure = run(
        spread_out,
        stack_of(jnp.bfloat16),
        1 << 22,
        4 << 20,
        SENT,
        in_specs=[VMEM] * 6,
        out_specs=HBM,
    )(base, *around)
    grad_rows, grad_channels, grad_point = run(
        finish,
        [jax.ShapeDtypeStruct(shape, jnp.float32) for shape in ((16, 128), (16, 16), (16, 16))],
        1 << 18,
        1 << 18,
    )(products, their_products, placed)
    return (
        response.reshape(pressure.shape),
        grad_pressure.reshape(pressure.shape),
        grad_rows.T,
        grad_channels,
        grad_point,
    )


def solution(mesh):
    return jax.shard_map(
        shards,
        mesh=mesh,
        in_specs=(P("gx", "gy", None, None), P("gx", "gy", None, None), P(), P(), P()),
        out_specs=(P("gx", "gy", None, None), P("gx", "gy", None, None), P(None, "gy"), P(), P()),
        check_vma=False,
    )
```

```python
import jax
import jax.numpy as jnp
import numpy as np
from jax import lax
from jax.experimental import pallas as pl
from jax.experimental.pallas import tpu as pltpu
from jax.sharding import PartitionSpec as P

DEPTH = 128
LEVELS = 4
PLANES = 16
LINES = 16
CH = 16
N_GY = 8
RING = 4
ROWS = 64
LIMIT = 12
GELU_A = float(np.sqrt(2.0 / np.pi))
GELU_B = 0.044715 * GELU_A
SHIFTS = (-1, 0, 1, 2)

HIGH = lax.Precision.HIGHEST


def lift_rows(rows):
    even, odd = rows[:, 0::2], rows[:, 1::2]
    detail = odd - 0.5 * (even + np.roll(even, -1, 1))
    smooth = even + 0.25 * (np.roll(detail, 1, 1) + detail)
    return smooth, detail


def depth_table():
    table = np.eye(DEPTH)
    for level in range(LEVELS):
        width = DEPTH >> level
        smooth, detail = lift_rows(table[:, :width])
        table = np.concatenate([smooth, detail, table[:, width:]], 1)
    return table


def plane_weights():
    total = 8 * PLANES
    table = np.eye(total)
    for level in range(LEVELS):
        table = lift_rows(table)[0]
    own = table[3 * PLANES : 4 * PLANES]
    return np.stack([own[:, 3 + shift] for shift in SHIFTS])


TABLE = depth_table()
ANALYSE = TABLE.astype(np.float32)
SYNTHESISE = np.linalg.inv(TABLE).astype(np.float32)
WEIGHTS = plane_weights().astype(np.float32)
RISE = (np.arange(PLANES) / PLANES).astype(np.float32)


def moved(block, distance):
    size = lax.axis_size("gx")
    return lax.ppermute(block, "gx", [(i, (i + distance) % size) for i in range(size)])


def routed(block, *hops):
    size = lax.axis_size("gx")
    route = [(i, (i + hops[i % 2]) % size) for i in range(size)]
    return lax.ppermute(block, "gx", route)


def across(block):
    return lax.ppermute(block, "gy", [(i, (i + RING) % N_GY) for i in range(N_GY)])


def along(block, distance):
    route = [(i, i // RING * RING + (i + distance) % RING) for i in range(N_GY)]
    return lax.ppermute(block, "gy", route)


def plane_sums(field_ref, own_ref, inner_ref, outer_ref, even_ref, odd_ref):
    odd = lax.rem(lax.axis_index("gx"), 2) == 1
    for first in range(0, LINES * CH, 32):
        rows = pl.ds(first, 32)
        sums = [None] * 4
        for j in range(PLANES):
            plane = field_ref[j, rows, :].astype(jnp.float32)
            for k in range(4):
                if WEIGHTS[k, j] != 0.0:
                    term = plane * float(WEIGHTS[k, j])
                    sums[k] = term if sums[k] is None else sums[k] + term
        own_ref[rows, :] = sums[1]
        inner_ref[rows, :] = jnp.where(odd, sums[0], sums[2])
        outer_ref[rows, :] = jnp.where(odd, sums[2], sums[0])
        even_ref[rows, :] = jnp.where(odd, 0.0, sums[3])
        odd_ref[rows, :] = jnp.where(odd, sums[3], 0.0)


def prepare(table_ref, point_ref, after_ref, kept_ref, map_ref, turned_ref):
    kept_ref[...] = table_ref[...]
    at_row = lax.broadcasted_iota(jnp.int32, (ROWS, CH), 0)
    at_column = lax.broadcasted_iota(jnp.int32, (ROWS, CH), 1)
    tall = (lax.rem(at_row, CH) == at_column).astype(jnp.bfloat16)
    at_row = lax.broadcasted_iota(jnp.int32, (ROWS, ROWS), 0)
    at_column = lax.broadcasted_iota(jnp.int32, (ROWS, ROWS), 1)
    same = at_row // CH == at_column // CH
    point = point_ref[...]
    for turn, dims in enumerate(((1, 0), (1, 1))):
        mapped = lax.dot_general(
            tall, point, (((dims[0],), (dims[1],)), ((), ())), preferred_element_type=jnp.float32
        )
        mapped = lax.dot_general(
            mapped.astype(jnp.bfloat16), tall, (((1,), (1,)), ((), ())), preferred_element_type=jnp.float32
        )
        mapped = jnp.where(same, mapped, 0.0).astype(jnp.bfloat16)
        if turn:
            turned_ref[...] = jnp.concatenate([mapped, mapped], 1)
        else:
            map_ref[...] = mapped


def combine(table_ref, *refs):
    total = sum(ref[...] for ref in refs[:-1])
    refs[-1][...] = jnp.dot(total, table_ref[...], precision=HIGH, preferred_element_type=jnp.float32)


def point_map(point_ref, field_ref, cotangent_ref, out_ref, field_kept_ref, cotangent_kept_ref):
    point = point_ref[...]

    @pl.loop(0, STEPS)
    def _(step):
        rows = pl.ds(pl.multiple_of(step * ROWS, ROWS), ROWS)
        for j in range(0, PLANES, 2):
            pair = jnp.concatenate([field_ref[j, rows, :], field_ref[j + 1, rows, :]], 1)
            mapped = jnp.dot(point, pair, preferred_element_type=jnp.float32) + pair.astype(jnp.float32)
            for n in range(2):
                out_ref[j + n, rows, :] = mapped[:, n * DEPTH : n * DEPTH + DEPTH]
                field_kept_ref[j + n, rows, :] = field_ref[j + n, rows, :]
                cotangent_kept_ref[j + n, rows, :] = cotangent_ref[j + n, rows, :]


def activate(
    turned_ref, mapped_ref, field_ref, cotangent_ref, delta_ref, after_ref,
    response_ref, base_ref, here_ref, up_ref, grad_ref, kept_ref, g_ref, acc_ref, sems,
):
    def chunk(step):
        rows = pl.ds(step * ROWS, ROWS)
        return pltpu.make_async_copy(kept_ref.at[:, rows, :], response_ref.at[:, rows, :], sems.at[step])

    turned = turned_ref[...]
    acc_ref[...] = jnp.zeros_like(acc_ref)
    for step in range(STEPS):
        for first in range(0, ROWS, 32):
            rows = pl.ds(step * ROWS + first, 32)
            delta = delta_ref[rows, :]
            slope = (after_ref[rows, :] - delta) * (1.0 / PLANES)
            base = delta + slope * float(PLANES)
            total = jnp.zeros_like(delta)
            up = jnp.zeros_like(delta)
            for at in range(PLANES - 1, -1, -1):
                base = base - slope
                value = mapped_ref[at, rows, :] + base
                square = value * value
                half = 0.5 + 0.5 * jnp.tanh(value * (GELU_A + GELU_B * square))
                active = value * half
                kept_ref[at, rows, :] = active.astype(jnp.bfloat16)
                rate = half + (active * (1.0 - half)) * (2.0 * GELU_A + 6.0 * GELU_B * square)
                g_pre = rate * cotangent_ref[at, rows, :].astype(jnp.float32)
                g_ref[at, pl.ds(first, 32), :] = g_pre
                total = total + g_pre
                if at:
                    up = up + total
            up = up * (1.0 / PLANES)
            here_ref[rows, :] = total - up
            up_ref[rows, :] = up
        chunk(step).start()
        rows = pl.ds(step * ROWS, ROWS)
        acc = acc_ref[...]
        for j in range(PLANES):
            g_pre = g_ref[j]
            high = g_pre.astype(jnp.bfloat16)
            low = (g_pre - high.astype(jnp.float32)).astype(jnp.bfloat16)
            base_ref[j, rows, :] = g_pre + jnp.dot(
                turned, jnp.concatenate([high, low], 0), preferred_element_type=jnp.float32
            )
            plane = field_ref[j, rows, :]
            acc = acc + lax.dot_general(
                jnp.concatenate([high, low], 1),
                jnp.concatenate([plane, plane], 1),
                (((1,), (1,)), ((), ())),
                preferred_element_type=jnp.float32,
            )
        acc_ref[...] = acc

    row = lax.broadcasted_iota(jnp.int32, (ROWS, ROWS), 0)
    column = lax.broadcasted_iota(jnp.int32, (ROWS, ROWS), 1)
    kept = jnp.where(row // CH == column // CH, acc_ref[...], 0.0)
    folded = kept[0:CH]
    for n in range(1, ROWS // CH):
        folded = folded + kept[n * CH : n * CH + CH]
    source = lax.broadcasted_iota(jnp.int32, (ROWS, DEPTH), 0)
    target = lax.broadcasted_iota(jnp.int32, (ROWS, DEPTH), 1)
    fold = (lax.rem(source, CH) + CH == target).astype(jnp.float32)
    grad_ref[...] = jnp.dot(folded, fold, precision=HIGH, preferred_element_type=jnp.float32)
    for step in range(STEPS):
        chunk(step).wait()


def halves(values):
    high = values.astype(jnp.bfloat16)
    return high, (values - high.astype(jnp.float32)).astype(jnp.bfloat16)


def row_products(own_ref, other_ref, after_ref, *refs):
    out_ref, pieces = refs[-1], refs[:-1]
    total = jnp.zeros((2 * LINES, RING * LINES), jnp.float32)
    for c in range(CH):
        lines = pl.ds(c, LINES, stride=CH)
        left, left_low = halves(jnp.concatenate([own_ref[lines, :], other_ref[lines, :]], 0))
        right, right_low = halves(jnp.concatenate([ref[lines, :] for ref in pieces], 0))
        total = total + lax.dot_general(
            jnp.concatenate([left, left, left_low], 1),
            jnp.concatenate([right, right_low, right], 1),
            (((1,), (1,)), ((), ())),
            preferred_element_type=jnp.float32,
        )
    small = pl.ds(LINES * CH, CH)
    products = jnp.concatenate([total[:LINES], total[LINES:]], 1)
    sums = sum(ref[small, :] for ref in pieces)
    sums = jnp.concatenate([sums[4 * n : 4 * n + 4, 0:32] for n in range(4)], 1)
    for n in range(PLANES):
        out_ref[n, 0:LINES, :] = products
        out_ref[n, LINES : LINES + 4, :] = sums


def spread_out(base_ref, own_ref, inner_ref, outer_ref, even_ref, odd_ref, out_ref, kept_ref, sems):
    odd = lax.rem(lax.axis_index("gx"), 2) == 1

    def chunk(step):
        rows = pl.ds(step * ROWS, ROWS)
        return pltpu.make_async_copy(kept_ref.at[:, rows, :], out_ref.at[:, rows, :], sems.at[step])

    for step in range(STEPS):
        for first in range(step * ROWS, (step + 1) * ROWS, 32):
            rows = pl.ds(first, 32)
            inner, outer = inner_ref[rows, :], outer_ref[rows, :]
            around = [
                jnp.where(odd, inner, outer),
                own_ref[rows, :],
                jnp.where(odd, outer, inner),
                jnp.where(odd, odd_ref[rows, :], even_ref[rows, :]),
            ]
            for j in range(PLANES):
                total = base_ref[j, rows, :]
                for k in range(4):
                    if WEIGHTS[k, j] != 0.0:
                        total = total + around[k] * float(WEIGHTS[k, j])
                kept_ref[j, rows, :] = total.astype(jnp.bfloat16)
        chunk(step).start()
    for step in range(STEPS):
        chunk(step).wait()


STEPS = LINES * CH // ROWS


def plane_of(kind):
    return jax.ShapeDtypeStruct((LINES * CH, DEPTH), kind)


def stack_of(kind):
    return jax.ShapeDtypeStruct((PLANES, LINES * CH, DEPTH), kind)


def add_up(parts_ref, out_ref):
    total = parts_ref[0]
    for n in range(1, PLANES):
        total = total + parts_ref[n]
    out_ref[...] = total


def finish(own_ref, their_ref, placed_ref, rows_ref, channels_ref, point_ref):
    joined = jnp.concatenate([own_ref[0:LINES, 0:64], their_ref[0:LINES, 64:128]], 1)
    rows_ref[...] = jnp.dot(joined, placed_ref[...], precision=HIGH, preferred_element_type=jnp.float32)
    small = own_ref[LINES : LINES + 4, :] + their_ref[LINES : LINES + 4, :]
    for n in range(4):
        channels_ref[4 * n : 4 * n + 4, :] = small[:, 32 * n : 32 * n + CH]
        point_ref[4 * n : 4 * n + 4, :] = small[:, 32 * n + CH : 32 * n + 2 * CH]


VMEM = pl.BlockSpec()
HBM = pl.BlockSpec(memory_space=pltpu.HBM)
ANY = pl.BlockSpec(memory_space=pl.ANY)
SENT = [pltpu.VMEM((PLANES, LINES * CH, DEPTH), jnp.bfloat16), pltpu.SemaphoreType.DMA((STEPS,))]


def run(kernel, out_shape, flops, size, scratch=(), **where):
    return pl.pallas_call(
        kernel,
        out_shape=out_shape,
        scratch_shapes=scratch,
        cost_estimate=pl.CostEstimate(flops=flops, bytes_accessed=size, transcendentals=0),
        compiler_params=pltpu.CompilerParams(vmem_limit_bytes=LIMIT * 1024 * 1024),
        **where,
    )


def shards(pressure, cotangent, mix_rows, mix_channels, pointwise):
    me = lax.axis_index("gy")
    side, spot = me // RING, lax.rem(me, RING)
    rows_w = mix_rows.astype(jnp.float32)
    channel_w = mix_channels.astype(jnp.float32)
    field = pressure.reshape(PLANES, LINES * CH, DEPTH)
    upstream = cotangent.reshape(PLANES, LINES * CH, DEPTH)

    def block(k_side, k_spot, y_side, y_spot):
        k_at = (k_side * RING + lax.rem(k_spot + RING, RING)) * LINES
        y_at = (y_side * RING + lax.rem(y_spot + RING, RING)) * LINES
        return lax.dynamic_slice(rows_w, (k_at, y_at), (LINES, LINES))

    own, inner, outer, even, odd = run(plane_sums, [plane_of(jnp.float32)] * 5, 1 << 22, 3 << 19)(field)
    table, point, turned = run(
        prepare,
        [
            jax.ShapeDtypeStruct((DEPTH, DEPTH), jnp.float32),
            jax.ShapeDtypeStruct((ROWS, ROWS), jnp.bfloat16),
            jax.ShapeDtypeStruct((ROWS, 2 * ROWS), jnp.bfloat16),
        ],
        1 << 20,
        1 << 18,
        in_specs=[VMEM, VMEM, ANY],
    )(jnp.asarray(ANALYSE), pointwise, own)
    passed = routed(even, 1, -1)
    far = routed(odd, 0, 2)
    coarse = run(combine, plane_of(jnp.float32), 1 << 23, 1 << 19)(
        table, own, routed(inner, 1, -1), routed(outer + passed, -1, 1), far
    ).reshape(LINES, CH, DEPTH)
    point_values, field, upstream = run(
        point_map,
        [stack_of(jnp.float32), stack_of(jnp.bfloat16), stack_of(jnp.bfloat16)],
        1 << 26,
        7 << 20,
    )(point, field, upstream)
    other = across(coarse)

    spread_spots = (2, 1, 3, 0)

    def blocks_for(y_side):
        return jnp.concatenate([block(side, spot + d, y_side, spot) for d in spread_spots], 0)

    own_mix = jnp.einsum("ky,ycz->kcz", blocks_for(side), coarse, precision=HIGH)
    own_mix = own_mix.reshape(RING, LINES, CH, DEPTH)
    partial = [
        own_mix[n] + jnp.einsum("ky,ycz->kcz", block(side, spot + d, 1 - side, spot), other, precision=HIGH)
        for n, d in enumerate(spread_spots)
    ]
    row_mixed = partial[3]
    for n in range(RING - 1):
        row_mixed = row_mixed + along(partial[n], spread_spots[n])
    mixed = jnp.einsum("dc,kcz->kdz", channel_w, row_mixed, precision=HIGH)
    delta = jnp.matmul(mixed - coarse, SYNTHESISE, precision=HIGH)
    after = moved(delta, -1)

    response, base, here, up, part_point = run(
        activate,
        [
            stack_of(jnp.bfloat16),
            stack_of(jnp.float32),
            plane_of(jnp.float32),
            plane_of(jnp.float32),
            jax.ShapeDtypeStruct((CH, DEPTH), jnp.float32),
        ],
        1 << 28,
        5 << 20,
        [
            SENT[0],
            pltpu.VMEM((PLANES, ROWS, DEPTH), jnp.float32),
            pltpu.VMEM((ROWS, ROWS), jnp.float32),
            SENT[1],
        ],
        in_specs=[VMEM] * 6,
        out_specs=[HBM, VMEM, VMEM, VMEM, VMEM],
    )(turned, point_values, field, upstream, delta.reshape(-1, DEPTH), after.reshape(-1, DEPTH))

    below = moved(up, 1)
    g_mixed = jnp.matmul((here + below).reshape(LINES, CH, DEPTH), SYNTHESISE.T, precision=HIGH)
    part_channels = jnp.einsum("kdz,kcz->dc", g_mixed, row_mixed, precision=HIGH)
    g_chan = jnp.einsum("dc,kdz->kcz", channel_w, g_mixed, precision=HIGH)
    small = part_point + jnp.pad(part_channels, ((0, 0), (0, DEPTH - CH)))
    packed = jnp.concatenate([g_chan.reshape(256, 128), small], 0)
    pieces = [packed] + [along(packed, d) for d in (2, 1, 3)]
    planes = [piece[:256].reshape(16, 16, 128) for piece in pieces]
    back = (0, 2, 1, 3)

    def partial_lines(y_side):
        return sum(
            jnp.einsum("ky,kcz->ycz", block(side, spot - d, y_side, spot), plane, precision=HIGH)
            for d, plane in zip(back, planes)
        )

    for_them = partial_lines(1 - side)
    far = across(for_them)
    products = run(
        row_products,
        jax.ShapeDtypeStruct((PLANES, 24, 128), jnp.float32),
        1 << 25,
        1 << 20,
        in_specs=[VMEM, VMEM, ANY] + [VMEM] * RING,
    )(coarse.reshape(256, 128), other.reshape(256, 128), for_them, *pieces)
    products = run(add_up, jax.ShapeDtypeStruct((24, 128), jnp.float32), 1 << 16, 1 << 18)(
        lax.all_to_all(products, "gx", 0, 0)
    )
    their_products = across(products)
    g_coarse = partial_lines(side) + far
    spread = jnp.matmul(g_coarse - g_mixed, ANALYSE.T, precision=HIGH).reshape(256, 128)
    far = routed(spread, 0, -2)
    outer = routed(spread, -1, 1)
    around = [spread, routed(spread, 1, -1), outer, routed(outer, 1, -1), far]
    at = lax.broadcasted_iota(jnp.int32, (128, 128), 0)
    turn = jnp.asarray(np.repeat(np.array(back * 2), 16))[:, None]
    k_side = jnp.where(at < 64, side, 1 - side)
    k_at = (k_side * RING + lax.rem(spot - turn + RING, RING)) * LINES + lax.rem(at, LINES)
    placed = (k_at == lax.broadcasted_iota(jnp.int32, (128, 128), 1)).astype(jnp.float32)
    grad_pressure = run(
        spread_out,
        stack_of(jnp.bfloat16),
        1 << 22,
        4 << 20,
        SENT,
        in_specs=[VMEM] * 6,
        out_specs=HBM,
    )(base, *around)
    grad_rows, grad_channels, grad_point = run(
        finish,
        [jax.ShapeDtypeStruct(shape, jnp.float32) for shape in ((16, 128), (16, 16), (16, 16))],
        1 << 18,
        1 << 18,
    )(products, their_products, placed)
    return (
        response.reshape(pressure.shape),
        grad_pressure.reshape(pressure.shape),
        grad_rows.T,
        grad_channels,
        grad_point,
    )


def solution(mesh):
    return jax.shard_map(
        shards,
        mesh=mesh,
        in_specs=(P("gx", "gy", None, None), P("gx", "gy", None, None), P(), P(), P()),
        out_specs=(P("gx", "gy", None, None), P("gx", "gy", None, None), P(None, "gy"), P(), P()),
        check_vma=False,
    )
```

```python
import jax
import jax.numpy as jnp
import numpy as np
from jax import lax
from jax.experimental import pallas as pl
from jax.experimental.pallas import tpu as pltpu
from jax.sharding import PartitionSpec as P

DEPTH = 128
LEVELS = 4
PLANES = 16
LINES = 16
CH = 16
N_GY = 8
RING = 4
AHEAD = (2, 1, 3, 0)
BEHIND = (0, -2, -1, -3)
ROWS = 64
LIMIT = 12
GELU_A = float(np.sqrt(2.0 / np.pi))
GELU_B = 0.044715 * GELU_A
SHIFTS = (-1, 0, 1, 2)

HIGH = lax.Precision.HIGHEST


def lift_rows(rows):
    even, odd = rows[:, 0::2], rows[:, 1::2]
    detail = odd - 0.5 * (even + np.roll(even, -1, 1))
    smooth = even + 0.25 * (np.roll(detail, 1, 1) + detail)
    return smooth, detail


def depth_table():
    table = np.eye(DEPTH)
    for level in range(LEVELS):
        width = DEPTH >> level
        smooth, detail = lift_rows(table[:, :width])
        table = np.concatenate([smooth, detail, table[:, width:]], 1)
    return table


def plane_weights():
    total = 8 * PLANES
    table = np.eye(total)
    for level in range(LEVELS):
        table = lift_rows(table)[0]
    own = table[3 * PLANES : 4 * PLANES]
    return np.stack([own[:, 3 + shift] for shift in SHIFTS])


TABLE = depth_table()
ANALYSE = TABLE.astype(np.float32)
SYNTHESISE = np.linalg.inv(TABLE).astype(np.float32)
WEIGHTS = plane_weights().astype(np.float32)
RISE = (np.arange(PLANES) / PLANES).astype(np.float32)


def moved(block, distance):
    size = lax.axis_size("gx")
    return lax.ppermute(block, "gx", [(i, (i + distance) % size) for i in range(size)])


def routed(block, *hops):
    size = lax.axis_size("gx")
    route = [(i, (i + hops[i % 2]) % size) for i in range(size)]
    return lax.ppermute(block, "gx", route)


def across(block):
    return lax.ppermute(block, "gy", [(i, (i + RING) % N_GY) for i in range(N_GY)])


def along(block, distance):
    route = [(i, i // RING * RING + (i + distance) % RING) for i in range(N_GY)]
    return lax.ppermute(block, "gy", route)


def plane_sums(field_ref, own_ref, inner_ref, outer_ref, far_ref):
    odd = lax.rem(lax.axis_index("gx"), 2) == 1
    for first in range(0, LINES * CH, 32):
        rows = pl.ds(first, 32)
        sums = [None] * 4
        for j in range(PLANES):
            plane = field_ref[j, rows, :].astype(jnp.float32)
            for k in range(4):
                if WEIGHTS[k, j] != 0.0:
                    term = plane * float(WEIGHTS[k, j])
                    sums[k] = term if sums[k] is None else sums[k] + term
        own_ref[rows, :] = sums[1]
        inner_ref[rows, :] = jnp.where(odd, sums[0], sums[2])
        outer_ref[rows, :] = jnp.where(odd, sums[2], sums[0])
        far_ref[rows, :] = sums[3]


def prepare(table_ref, point_ref, rows_ref, after_ref, kept_ref, map_ref, turned_ref, ahead_ref, behind_ref):
    kept_ref[...] = table_ref[...]
    at_row = lax.broadcasted_iota(jnp.int32, (ROWS, CH), 0)
    at_column = lax.broadcasted_iota(jnp.int32, (ROWS, CH), 1)
    tall = (lax.rem(at_row, CH) == at_column).astype(jnp.bfloat16)
    at_row = lax.broadcasted_iota(jnp.int32, (ROWS, ROWS), 0)
    at_column = lax.broadcasted_iota(jnp.int32, (ROWS, ROWS), 1)
    same = at_row // CH == at_column // CH
    point = point_ref[...]
    for turn, dims in enumerate(((1, 0), (1, 1))):
        mapped = lax.dot_general(
            tall, point, (((dims[0],), (dims[1],)), ((), ())), preferred_element_type=jnp.float32
        )
        mapped = lax.dot_general(
            mapped.astype(jnp.bfloat16), tall, (((1,), (1,)), ((), ())), preferred_element_type=jnp.float32
        )
        mapped = jnp.where(same, mapped, 0.0).astype(jnp.bfloat16)
        if turn:
            turned_ref[...] = jnp.concatenate([mapped, mapped], 1)
        else:
            map_ref[...] = mapped

    me = lax.axis_index("gy")
    side, spot = me // RING, lax.rem(me, RING)

    def chosen(count, first_side, steps):
        row = lax.broadcasted_iota(jnp.int32, (count, 128), 0)
        column = lax.broadcasted_iota(jnp.int32, (count, 128), 1)
        step = jnp.zeros_like(row)
        for n, distance in enumerate(steps):
            step = jnp.where(row // LINES == n, distance, step)
        at = (first_side * RING + lax.rem(spot + step + RING, RING)) * LINES + lax.rem(row, LINES)
        return (at == column).astype(jnp.bfloat16)

    lines = jnp.concatenate([chosen(LINES, side, (0,)), chosen(LINES, 1 - side, (0,))], 0)
    for ref, steps in ((ahead_ref, AHEAD), (behind_ref, BEHIND)):
        taken = jnp.dot(chosen(RING * LINES, side, steps), rows_ref[...], preferred_element_type=jnp.float32)
        ref[...] = lax.dot_general(
            taken.astype(jnp.bfloat16), lines, (((1,), (1,)), ((), ())), preferred_element_type=jnp.float32
        )


def combine(table_ref, *refs):
    total = sum(ref[...] for ref in refs[:-1])
    refs[-1][...] = jnp.dot(total, table_ref[...], precision=HIGH, preferred_element_type=jnp.float32)


def point_map(point_ref, field_ref, cotangent_ref, out_ref, field_kept_ref, cotangent_kept_ref):
    point = point_ref[...]

    @pl.loop(0, STEPS)
    def _(step):
        rows = pl.ds(pl.multiple_of(step * ROWS, ROWS), ROWS)
        for j in range(0, PLANES, 2):
            pair = jnp.concatenate([field_ref[j, rows, :], field_ref[j + 1, rows, :]], 1)
            mapped = jnp.dot(point, pair, preferred_element_type=jnp.float32) + pair.astype(jnp.float32)
            for n in range(2):
                out_ref[j + n, rows, :] = mapped[:, n * DEPTH : n * DEPTH + DEPTH]
                field_kept_ref[j + n, rows, :] = field_ref[j + n, rows, :]
                cotangent_kept_ref[j + n, rows, :] = cotangent_ref[j + n, rows, :]


def activate(
    turned_ref, mapped_ref, field_ref, cotangent_ref, delta_ref, after_ref,
    response_ref, base_ref, here_ref, up_ref, grad_ref, kept_ref, g_ref, acc_ref, sems,
):
    def chunk(step):
        rows = pl.ds(step * ROWS, ROWS)
        return pltpu.make_async_copy(kept_ref.at[:, rows, :], response_ref.at[:, rows, :], sems.at[step])

    turned = turned_ref[...]
    acc_ref[...] = jnp.zeros_like(acc_ref)
    for step in range(STEPS):
        for first in range(0, ROWS, 32):
            rows = pl.ds(step * ROWS + first, 32)
            delta = delta_ref[rows, :]
            slope = (after_ref[rows, :] - delta) * (1.0 / PLANES)
            base = delta + slope * float(PLANES)
            total = jnp.zeros_like(delta)
            up = jnp.zeros_like(delta)
            for at in range(PLANES - 1, -1, -1):
                base = base - slope
                value = mapped_ref[at, rows, :] + base
                square = value * value
                half = 0.5 + 0.5 * jnp.tanh(value * (GELU_A + GELU_B * square))
                active = value * half
                kept_ref[at, rows, :] = active.astype(jnp.bfloat16)
                rate = half + (active * (1.0 - half)) * (2.0 * GELU_A + 6.0 * GELU_B * square)
                g_pre = rate * cotangent_ref[at, rows, :].astype(jnp.float32)
                g_ref[at, pl.ds(first, 32), :] = g_pre
                total = total + g_pre
                if at:
                    up = up + total
            up = up * (1.0 / PLANES)
            here_ref[rows, :] = total - up
            up_ref[rows, :] = up
        chunk(step).start()
        rows = pl.ds(step * ROWS, ROWS)
        acc = acc_ref[...]
        for j in range(PLANES):
            g_pre = g_ref[j]
            high = g_pre.astype(jnp.bfloat16)
            low = (g_pre - high.astype(jnp.float32)).astype(jnp.bfloat16)
            base_ref[j, rows, :] = g_pre + jnp.dot(
                turned, jnp.concatenate([high, low], 0), preferred_element_type=jnp.float32
            )
            plane = field_ref[j, rows, :]
            acc = acc + lax.dot_general(
                jnp.concatenate([high, low], 1),
                jnp.concatenate([plane, plane], 1),
                (((1,), (1,)), ((), ())),
                preferred_element_type=jnp.float32,
            )
        acc_ref[...] = acc

    row = lax.broadcasted_iota(jnp.int32, (ROWS, ROWS), 0)
    column = lax.broadcasted_iota(jnp.int32, (ROWS, ROWS), 1)
    kept = jnp.where(row // CH == column // CH, acc_ref[...], 0.0)
    folded = kept[0:CH]
    for n in range(1, ROWS // CH):
        folded = folded + kept[n * CH : n * CH + CH]
    source = lax.broadcasted_iota(jnp.int32, (ROWS, DEPTH), 0)
    target = lax.broadcasted_iota(jnp.int32, (ROWS, DEPTH), 1)
    fold = (lax.rem(source, CH) + CH == target).astype(jnp.float32)
    grad_ref[...] = jnp.dot(folded, fold, precision=HIGH, preferred_element_type=jnp.float32)
    for step in range(STEPS):
        chunk(step).wait()


def halves(values):
    high = values.astype(jnp.bfloat16)
    return high, (values - high.astype(jnp.float32)).astype(jnp.bfloat16)


def row_products(own_ref, other_ref, after_ref, *refs):
    out_ref, pieces = refs[-1], refs[:-1]
    total = jnp.zeros((2 * LINES, RING * LINES), jnp.float32)
    for c in range(CH):
        lines = pl.ds(c, LINES, stride=CH)
        left, left_low = halves(jnp.concatenate([own_ref[lines, :], other_ref[lines, :]], 0))
        right, right_low = halves(jnp.concatenate([ref[lines, :] for ref in pieces], 0))
        total = total + lax.dot_general(
            jnp.concatenate([left, left, left_low], 1),
            jnp.concatenate([right, right_low, right], 1),
            (((1,), (1,)), ((), ())),
            preferred_element_type=jnp.float32,
        )
    small = pl.ds(LINES * CH, CH)
    products = jnp.concatenate([total[:LINES], total[LINES:]], 1)
    sums = sum(ref[small, :] for ref in pieces)
    sums = jnp.concatenate([sums[4 * n : 4 * n + 4, 0:32] for n in range(4)], 1)
    for n in range(PLANES):
        out_ref[n, 0:LINES, :] = products
        out_ref[n, LINES : LINES + 4, :] = sums


def spread_out(base_ref, far_ref, outer_ref, inner_ref, own_ref, out_ref, kept_ref, sems):
    odd = lax.rem(lax.axis_index("gx"), 2) == 1

    def chunk(step):
        rows = pl.ds(step * ROWS, ROWS)
        return pltpu.make_async_copy(kept_ref.at[:, rows, :], out_ref.at[:, rows, :], sems.at[step])

    for step in range(STEPS):
        for first in range(step * ROWS, (step + 1) * ROWS, 32):
            rows = pl.ds(first, 32)
            inner, outer = inner_ref[rows, :], outer_ref[rows, :]
            around = [
                jnp.where(odd, inner, outer),
                own_ref[rows, :],
                jnp.where(odd, outer, inner),
                far_ref[rows, :],
            ]
            for j in range(PLANES):
                total = base_ref[j, rows, :]
                for k in range(4):
                    if WEIGHTS[k, j] != 0.0:
                        total = total + around[k] * float(WEIGHTS[k, j])
                kept_ref[j, rows, :] = total.astype(jnp.bfloat16)
        chunk(step).start()
    for step in range(STEPS):
        chunk(step).wait()


STEPS = LINES * CH // ROWS


def plane_of(kind):
    return jax.ShapeDtypeStruct((LINES * CH, DEPTH), kind)


def stack_of(kind):
    return jax.ShapeDtypeStruct((PLANES, LINES * CH, DEPTH), kind)


def add_up(parts_ref, out_ref):
    total = parts_ref[0]
    for n in range(1, PLANES):
        total = total + parts_ref[n]
    out_ref[...] = total


def finish(own_ref, their_ref, placed_ref, rows_ref, channels_ref, point_ref):
    joined = jnp.concatenate([own_ref[0:LINES, 0:64], their_ref[0:LINES, 64:128]], 1)
    rows_ref[...] = jnp.dot(joined, placed_ref[...], precision=HIGH, preferred_element_type=jnp.float32)
    small = own_ref[LINES : LINES + 4, :] + their_ref[LINES : LINES + 4, :]
    for n in range(4):
        channels_ref[4 * n : 4 * n + 4, :] = small[:, 32 * n : 32 * n + CH]
        point_ref[4 * n : 4 * n + 4, :] = small[:, 32 * n + CH : 32 * n + 2 * CH]


VMEM = pl.BlockSpec()
HBM = pl.BlockSpec(memory_space=pltpu.HBM)
ANY = pl.BlockSpec(memory_space=pl.ANY)
SENT = [pltpu.VMEM((PLANES, LINES * CH, DEPTH), jnp.bfloat16), pltpu.SemaphoreType.DMA((STEPS,))]


def run(kernel, out_shape, flops, size, scratch=(), **where):
    return pl.pallas_call(
        kernel,
        out_shape=out_shape,
        scratch_shapes=scratch,
        cost_estimate=pl.CostEstimate(flops=flops, bytes_accessed=size, transcendentals=0),
        compiler_params=pltpu.CompilerParams(vmem_limit_bytes=LIMIT * 1024 * 1024),
        **where,
    )


def shards(pressure, cotangent, mix_rows, mix_channels, pointwise):
    me = lax.axis_index("gy")
    side, spot = me // RING, lax.rem(me, RING)
    channel_w = mix_channels.astype(jnp.float32)
    field = pressure.reshape(PLANES, LINES * CH, DEPTH)
    upstream = cotangent.reshape(PLANES, LINES * CH, DEPTH)

    own, inner, outer, far = run(plane_sums, [plane_of(jnp.float32)] * 4, 1 << 22, 3 << 19)(field)
    table, point, turned, ahead, behind = run(
        prepare,
        [
            jax.ShapeDtypeStruct((DEPTH, DEPTH), jnp.float32),
            jax.ShapeDtypeStruct((ROWS, ROWS), jnp.bfloat16),
            jax.ShapeDtypeStruct((ROWS, 2 * ROWS), jnp.bfloat16),
            jax.ShapeDtypeStruct((RING * LINES, 2 * LINES), jnp.float32),
            jax.ShapeDtypeStruct((RING * LINES, 2 * LINES), jnp.float32),
        ],
        1 << 20,
        1 << 18,
        in_specs=[VMEM, VMEM, VMEM, ANY],
    )(jnp.asarray(ANALYSE), pointwise, mix_rows, own)
    far = routed(far, 2, 2)
    outer = routed(outer, -1, 1)
    inner = routed(inner, 1, -1)
    coarse = run(combine, plane_of(jnp.float32), 1 << 23, 1 << 19)(
        table, own, far, outer, inner
    ).reshape(LINES, CH, DEPTH)
    point_values, field, upstream = run(
        point_map,
        [stack_of(jnp.float32), stack_of(jnp.bfloat16), stack_of(jnp.bfloat16)],
        1 << 26,
        7 << 20,
    )(point, field, upstream)
    other = across(coarse)

    own_mix = jnp.einsum("ky,ycz->kcz", ahead[:, :LINES], coarse, precision=HIGH)
    own_mix = own_mix.reshape(RING, LINES, CH, DEPTH)
    far_weights = ahead[:, LINES:].reshape(RING, LINES, LINES)
    partial = [
        own_mix[n] + jnp.einsum("ky,ycz->kcz", far_weights[n], other, precision=HIGH) for n in range(RING)
    ]
    row_mixed = partial[3]
    for n in range(RING - 1):
        row_mixed = row_mixed + along(partial[n], AHEAD[n])
    mixed = jnp.einsum("dc,kcz->kdz", channel_w, row_mixed, precision=HIGH)
    delta = jnp.matmul(mixed - coarse, SYNTHESISE, precision=HIGH)
    after = moved(delta, -1)

    response, base, here, up, part_point = run(
        activate,
        [
            stack_of(jnp.bfloat16),
            stack_of(jnp.float32),
            plane_of(jnp.float32),
            plane_of(jnp.float32),
            jax.ShapeDtypeStruct((CH, DEPTH), jnp.float32),
        ],
        1 << 28,
        5 << 20,
        [
            SENT[0],
            pltpu.VMEM((PLANES, ROWS, DEPTH), jnp.float32),
            pltpu.VMEM((ROWS, ROWS), jnp.float32),
            SENT[1],
        ],
        in_specs=[VMEM] * 6,
        out_specs=[HBM, VMEM, VMEM, VMEM, VMEM],
    )(turned, point_values, field, upstream, delta.reshape(-1, DEPTH), after.reshape(-1, DEPTH))

    below = moved(up, 1)
    g_mixed = jnp.matmul((here + below).reshape(LINES, CH, DEPTH), SYNTHESISE.T, precision=HIGH)
    part_channels = jnp.einsum("kdz,kcz->dc", g_mixed, row_mixed, precision=HIGH)
    g_chan = jnp.einsum("dc,kdz->kcz", channel_w, g_mixed, precision=HIGH)
    small = part_point + jnp.pad(part_channels, ((0, 0), (0, DEPTH - CH)))
    packed = jnp.concatenate([g_chan.reshape(256, 128), small], 0)
    pieces = [packed] + [along(packed, -d) for d in BEHIND[1:]]
    planes = [piece[:256].reshape(16, 16, 128) for piece in pieces]

    def partial_lines(weights):
        weights = weights.reshape(RING, LINES, LINES)
        return sum(
            jnp.einsum("ky,kcz->ycz", weights[n], plane, precision=HIGH) for n, plane in enumerate(planes)
        )

    for_them = partial_lines(behind[:, LINES:])
    far = across(for_them)
    products = run(
        row_products,
        jax.ShapeDtypeStruct((PLANES, 24, 128), jnp.float32),
        1 << 25,
        1 << 20,
        in_specs=[VMEM, VMEM, ANY] + [VMEM] * RING,
    )(coarse.reshape(256, 128), other.reshape(256, 128), for_them, *pieces)
    products = run(add_up, jax.ShapeDtypeStruct((24, 128), jnp.float32), 1 << 16, 1 << 18)(
        lax.all_to_all(products, "gx", 0, 0)
    )
    their_products = across(products)
    g_coarse = partial_lines(behind[:, :LINES]) + far
    spread = jnp.matmul(g_coarse - g_mixed, ANALYSE.T, precision=HIGH).reshape(256, 128)
    far = routed(spread, -2, -2)
    outer = routed(spread, -1, 1)
    around = [far, outer, routed(spread, 1, -1), spread]
    at = lax.broadcasted_iota(jnp.int32, (128, 128), 0)
    turn = jnp.asarray(np.repeat(np.array(BEHIND * 2), 16))[:, None]
    k_side = jnp.where(at < 64, side, 1 - side)
    k_at = (k_side * RING + lax.rem(spot + turn + RING, RING)) * LINES + lax.rem(at, LINES)
    placed = (k_at == lax.broadcasted_iota(jnp.int32, (128, 128), 1)).astype(jnp.float32)
    grad_pressure = run(
        spread_out,
        stack_of(jnp.bfloat16),
        1 << 22,
        4 << 20,
        SENT,
        in_specs=[VMEM] * 5,
        out_specs=HBM,
    )(base, *around)
    grad_rows, grad_channels, grad_point = run(
        finish,
        [jax.ShapeDtypeStruct(shape, jnp.float32) for shape in ((16, 128), (16, 16), (16, 16))],
        1 << 18,
        1 << 18,
    )(products, their_products, placed)
    return (
        response.reshape(pressure.shape),
        grad_pressure.reshape(pressure.shape),
        grad_rows.T,
        grad_channels,
        grad_point,
    )


def solution(mesh):
    return jax.shard_map(
        shards,
        mesh=mesh,
        in_specs=(P("gx", "gy", None, None), P("gx", "gy", None, None), P(), P(), P()),
        out_specs=(P("gx", "gy", None, None), P("gx", "gy", None, None), P(None, "gy"), P(), P()),
        check_vma=False,
    )
```

```python
import jax
import jax.numpy as jnp
import numpy as np
from jax import lax
from jax.experimental import pallas as pl
from jax.experimental.pallas import tpu as pltpu
from jax.sharding import PartitionSpec as P

DEPTH = 128
LEVELS = 4
PLANES = 16
LINES = 16
CH = 16
N_GY = 8
RING = 4
AHEAD = (2, 1, 3, 0)
BEHIND = (0, -2, -1, -3)
ROWS = 64
LIMIT = 12
GELU_A = float(np.sqrt(2.0 / np.pi))
GELU_B = 0.044715 * GELU_A
SHIFTS = (-1, 0, 1, 2)

HIGH = lax.Precision.HIGHEST


def lift_rows(rows):
    even, odd = rows[:, 0::2], rows[:, 1::2]
    detail = odd - 0.5 * (even + np.roll(even, -1, 1))
    smooth = even + 0.25 * (np.roll(detail, 1, 1) + detail)
    return smooth, detail


def depth_table():
    table = np.eye(DEPTH)
    for level in range(LEVELS):
        width = DEPTH >> level
        smooth, detail = lift_rows(table[:, :width])
        table = np.concatenate([smooth, detail, table[:, width:]], 1)
    return table


def depth_back():
    table = np.eye(DEPTH)
    for level in reversed(range(LEVELS)):
        width = DEPTH >> level
        smooth, detail = table[:, : width // 2], table[:, width // 2 : width]
        even = smooth - 0.25 * (np.roll(detail, 1, 1) + detail)
        odd = detail + 0.5 * (even + np.roll(even, -1, 1))
        head = np.stack([even, odd], 2).reshape(DEPTH, width)
        table = np.concatenate([head, table[:, width:]], 1)
    return table


def plane_weights():
    total = 8 * PLANES
    table = np.eye(total)
    for level in range(LEVELS):
        table = lift_rows(table)[0]
    own = table[3 * PLANES : 4 * PLANES]
    return np.stack([own[:, 3 + shift] for shift in SHIFTS])


ANALYSE = depth_table().astype(np.float32)
SYNTHESISE = depth_back().astype(np.float32)
WEIGHTS = plane_weights().astype(np.float32)
RISE = (np.arange(PLANES) / PLANES).astype(np.float32)


def moved(block, distance):
    size = lax.axis_size("gx")
    return lax.ppermute(block, "gx", [(i, (i + distance) % size) for i in range(size)])


def routed(block, *hops):
    size = lax.axis_size("gx")
    route = [(i, (i + hops[i % 2]) % size) for i in range(size)]
    return lax.ppermute(block, "gx", route)


def across(block):
    return lax.ppermute(block, "gy", [(i, (i + RING) % N_GY) for i in range(N_GY)])


def along(block, distance):
    route = [(i, i // RING * RING + (i + distance) % RING) for i in range(N_GY)]
    return lax.ppermute(block, "gy", route)


def plane_sums(field_ref, own_ref, inner_ref, outer_ref, far_ref):
    odd = lax.rem(lax.axis_index("gx"), 2) == 1
    for first in range(0, LINES * CH, 32):
        rows = pl.ds(first, 32)
        sums = [None] * 4
        for j in range(PLANES):
            plane = field_ref[j, rows, :].astype(jnp.float32)
            for k in range(4):
                if WEIGHTS[k, j] != 0.0:
                    term = plane * float(WEIGHTS[k, j])
                    sums[k] = term if sums[k] is None else sums[k] + term
        own_ref[rows, :] = sums[1]
        inner_ref[rows, :] = jnp.where(odd, sums[0], sums[2])
        outer_ref[rows, :] = jnp.where(odd, sums[2], sums[0])
        far_ref[rows, :] = sums[3]


def prepare(table_ref, point_ref, rows_ref, after_ref, kept_ref, map_ref, turned_ref, ahead_ref, behind_ref):
    kept_ref[...] = table_ref[...]
    at_row = lax.broadcasted_iota(jnp.int32, (ROWS, CH), 0)
    at_column = lax.broadcasted_iota(jnp.int32, (ROWS, CH), 1)
    tall = (lax.rem(at_row, CH) == at_column).astype(jnp.bfloat16)
    at_row = lax.broadcasted_iota(jnp.int32, (ROWS, ROWS), 0)
    at_column = lax.broadcasted_iota(jnp.int32, (ROWS, ROWS), 1)
    same = at_row // CH == at_column // CH
    point = point_ref[...]
    for turn, dims in enumerate(((1, 0), (1, 1))):
        mapped = lax.dot_general(
            tall, point, (((dims[0],), (dims[1],)), ((), ())), preferred_element_type=jnp.float32
        )
        mapped = lax.dot_general(
            mapped.astype(jnp.bfloat16), tall, (((1,), (1,)), ((), ())), preferred_element_type=jnp.float32
        )
        mapped = jnp.where(same, mapped, 0.0).astype(jnp.bfloat16)
        if turn:
            turned_ref[...] = jnp.concatenate([mapped, mapped], 1)
        else:
            map_ref[...] = mapped

    me = lax.axis_index("gy")
    side, spot = me // RING, lax.rem(me, RING)

    def chosen(count, first_side, steps):
        row = lax.broadcasted_iota(jnp.int32, (count, 128), 0)
        column = lax.broadcasted_iota(jnp.int32, (count, 128), 1)
        step = jnp.zeros_like(row)
        for n, distance in enumerate(steps):
            step = jnp.where(row // LINES == n, distance, step)
        at = (first_side * RING + lax.rem(spot + step + RING, RING)) * LINES + lax.rem(row, LINES)
        return (at == column).astype(jnp.bfloat16)

    lines = jnp.concatenate([chosen(LINES, side, (0,)), chosen(LINES, 1 - side, (0,))], 0)
    for ref, steps in ((ahead_ref, AHEAD), (behind_ref, BEHIND)):
        taken = jnp.dot(chosen(RING * LINES, side, steps), rows_ref[...], preferred_element_type=jnp.float32)
        ref[...] = lax.dot_general(
            taken.astype(jnp.bfloat16), lines, (((1,), (1,)), ((), ())), preferred_element_type=jnp.float32
        )


def combine(table_ref, *refs):
    total = sum(ref[...] for ref in refs[:-1])
    refs[-1][...] = jnp.dot(total, table_ref[...], precision=HIGH, preferred_element_type=jnp.float32)


def point_map(point_ref, field_ref, cotangent_ref, out_ref, field_kept_ref, cotangent_kept_ref):
    point = point_ref[...]

    @pl.loop(0, STEPS)
    def _(step):
        rows = pl.ds(pl.multiple_of(step * ROWS, ROWS), ROWS)
        for j in range(0, PLANES, 2):
            pair = jnp.concatenate([field_ref[j, rows, :], field_ref[j + 1, rows, :]], 1)
            mapped = jnp.dot(point, pair, preferred_element_type=jnp.float32) + pair.astype(jnp.float32)
            for n in range(2):
                out_ref[j + n, rows, :] = mapped[:, n * DEPTH : n * DEPTH + DEPTH]
                field_kept_ref[j + n, rows, :] = field_ref[j + n, rows, :]
                cotangent_kept_ref[j + n, rows, :] = cotangent_ref[j + n, rows, :]


def activate(
    turned_ref, mapped_ref, field_ref, cotangent_ref, delta_ref, after_ref,
    response_ref, base_ref, here_ref, up_ref, grad_ref, kept_ref, g_ref, acc_ref, sems,
):
    def chunk(step):
        rows = pl.ds(step * ROWS, ROWS)
        return pltpu.make_async_copy(kept_ref.at[:, rows, :], response_ref.at[:, rows, :], sems.at[step])

    turned = turned_ref[...]
    acc_ref[...] = jnp.zeros_like(acc_ref)
    for step in range(STEPS):
        for first in range(0, ROWS, 32):
            rows = pl.ds(step * ROWS + first, 32)
            delta = delta_ref[rows, :]
            slope = (after_ref[rows, :] - delta) * (1.0 / PLANES)
            base = delta + slope * float(PLANES)
            total = jnp.zeros_like(delta)
            up = jnp.zeros_like(delta)
            for at in range(PLANES - 1, -1, -1):
                base = base - slope
                value = mapped_ref[at, rows, :] + base
                square = value * value
                half = 0.5 + 0.5 * jnp.tanh(value * (GELU_A + GELU_B * square))
                active = value * half
                kept_ref[at, rows, :] = active.astype(jnp.bfloat16)
                rate = half + (active * (1.0 - half)) * (2.0 * GELU_A + 6.0 * GELU_B * square)
                g_pre = rate * cotangent_ref[at, rows, :].astype(jnp.float32)
                g_ref[at, pl.ds(first, 32), :] = g_pre
                total = total + g_pre
                if at:
                    up = up + total
            up = up * (1.0 / PLANES)
            here_ref[rows, :] = total - up
            up_ref[rows, :] = up
        chunk(step).start()
        rows = pl.ds(step * ROWS, ROWS)
        acc = acc_ref[...]
        for j in range(PLANES):
            g_pre = g_ref[j]
            high = g_pre.astype(jnp.bfloat16)
            low = (g_pre - high.astype(jnp.float32)).astype(jnp.bfloat16)
            base_ref[j, rows, :] = g_pre + jnp.dot(
                turned, jnp.concatenate([high, low], 0), preferred_element_type=jnp.float32
            )
            plane = field_ref[j, rows, :]
            acc = acc + lax.dot_general(
                jnp.concatenate([high, low], 1),
                jnp.concatenate([plane, plane], 1),
                (((1,), (1,)), ((), ())),
                preferred_element_type=jnp.float32,
            )
        acc_ref[...] = acc

    row = lax.broadcasted_iota(jnp.int32, (ROWS, ROWS), 0)
    column = lax.broadcasted_iota(jnp.int32, (ROWS, ROWS), 1)
    kept = jnp.where(row // CH == column // CH, acc_ref[...], 0.0)
    folded = kept[0:CH]
    for n in range(1, ROWS // CH):
        folded = folded + kept[n * CH : n * CH + CH]
    source = lax.broadcasted_iota(jnp.int32, (ROWS, DEPTH), 0)
    target = lax.broadcasted_iota(jnp.int32, (ROWS, DEPTH), 1)
    fold = (lax.rem(source, CH) + CH == target).astype(jnp.float32)
    grad_ref[...] = jnp.dot(folded, fold, precision=HIGH, preferred_element_type=jnp.float32)
    for step in range(STEPS):
        chunk(step).wait()


def halves(values):
    high = values.astype(jnp.bfloat16)
    return high, (values - high.astype(jnp.float32)).astype(jnp.bfloat16)


def row_products(own_ref, other_ref, after_ref, *refs):
    out_ref, pieces = refs[-1], refs[:-1]
    total = jnp.zeros((2 * LINES, RING * LINES), jnp.float32)
    for c in range(CH):
        lines = pl.ds(c, LINES, stride=CH)
        left, left_low = halves(jnp.concatenate([own_ref[lines, :], other_ref[lines, :]], 0))
        right, right_low = halves(jnp.concatenate([ref[lines, :] for ref in pieces], 0))
        total = total + lax.dot_general(
            jnp.concatenate([left, left, left_low], 1),
            jnp.concatenate([right, right_low, right], 1),
            (((1,), (1,)), ((), ())),
            preferred_element_type=jnp.float32,
        )
    small = pl.ds(LINES * CH, CH)
    products = jnp.concatenate([total[:LINES], total[LINES:]], 1)
    sums = sum(ref[small, :] for ref in pieces)
    sums = jnp.concatenate([sums[4 * n : 4 * n + 4, 0:32] for n in range(4)], 1)
    for n in range(PLANES):
        out_ref[n, 0:LINES, :] = products
        out_ref[n, LINES : LINES + 4, :] = sums


def spread_out(base_ref, far_ref, outer_ref, inner_ref, own_ref, out_ref, kept_ref, sems):
    odd = lax.rem(lax.axis_index("gx"), 2) == 1

    def chunk(step):
        rows = pl.ds(step * ROWS, ROWS)
        return pltpu.make_async_copy(kept_ref.at[:, rows, :], out_ref.at[:, rows, :], sems.at[step])

    for step in range(STEPS):
        for first in range(step * ROWS, (step + 1) * ROWS, 32):
            rows = pl.ds(first, 32)
            inner, outer = inner_ref[rows, :], outer_ref[rows, :]
            around = [
                jnp.where(odd, inner, outer),
                own_ref[rows, :],
                jnp.where(odd, outer, inner),
                far_ref[rows, :],
            ]
            for j in range(PLANES):
                total = base_ref[j, rows, :]
                for k in range(4):
                    if WEIGHTS[k, j] != 0.0:
                        total = total + around[k] * float(WEIGHTS[k, j])
                kept_ref[j, rows, :] = total.astype(jnp.bfloat16)
        chunk(step).start()
    for step in range(STEPS):
        chunk(step).wait()


STEPS = LINES * CH // ROWS


def plane_of(kind):
    return jax.ShapeDtypeStruct((LINES * CH, DEPTH), kind)


def stack_of(kind):
    return jax.ShapeDtypeStruct((PLANES, LINES * CH, DEPTH), kind)


def add_up(parts_ref, out_ref):
    total = parts_ref[0]
    for n in range(1, PLANES):
        total = total + parts_ref[n]
    out_ref[...] = total


def finish(own_ref, their_ref, placed_ref, rows_ref, channels_ref, point_ref):
    joined = jnp.concatenate([own_ref[0:LINES, 0:64], their_ref[0:LINES, 64:128]], 1)
    rows_ref[...] = jnp.dot(joined, placed_ref[...], precision=HIGH, preferred_element_type=jnp.float32)
    small = own_ref[LINES : LINES + 4, :] + their_ref[LINES : LINES + 4, :]
    for n in range(4):
        channels_ref[4 * n : 4 * n + 4, :] = small[:, 32 * n : 32 * n + CH]
        point_ref[4 * n : 4 * n + 4, :] = small[:, 32 * n + CH : 32 * n + 2 * CH]


VMEM = pl.BlockSpec()
HBM = pl.BlockSpec(memory_space=pltpu.HBM)
ANY = pl.BlockSpec(memory_space=pl.ANY)
SENT = [pltpu.VMEM((PLANES, LINES * CH, DEPTH), jnp.bfloat16), pltpu.SemaphoreType.DMA((STEPS,))]


def run(kernel, out_shape, flops, size, scratch=(), **where):
    return pl.pallas_call(
        kernel,
        out_shape=out_shape,
        scratch_shapes=scratch,
        cost_estimate=pl.CostEstimate(flops=flops, bytes_accessed=size, transcendentals=0),
        compiler_params=pltpu.CompilerParams(vmem_limit_bytes=LIMIT * 1024 * 1024),
        **where,
    )


def shards(pressure, cotangent, mix_rows, mix_channels, pointwise):
    me = lax.axis_index("gy")
    side, spot = me // RING, lax.rem(me, RING)
    channel_w = mix_channels.astype(jnp.float32)
    field = pressure.reshape(PLANES, LINES * CH, DEPTH)
    upstream = cotangent.reshape(PLANES, LINES * CH, DEPTH)

    own, inner, outer, far = run(plane_sums, [plane_of(jnp.float32)] * 4, 1 << 22, 3 << 19)(field)
    table, point, turned, ahead, behind = run(
        prepare,
        [
            jax.ShapeDtypeStruct((DEPTH, DEPTH), jnp.float32),
            jax.ShapeDtypeStruct((ROWS, ROWS), jnp.bfloat16),
            jax.ShapeDtypeStruct((ROWS, 2 * ROWS), jnp.bfloat16),
            jax.ShapeDtypeStruct((RING * LINES, 2 * LINES), jnp.float32),
            jax.ShapeDtypeStruct((RING * LINES, 2 * LINES), jnp.float32),
        ],
        1 << 20,
        1 << 18,
        in_specs=[VMEM, VMEM, VMEM, ANY],
    )(jnp.asarray(ANALYSE), pointwise, mix_rows, own)
    far = routed(far, 2, 2)
    outer = routed(outer, -1, 1)
    inner = routed(inner, 1, -1)
    coarse = run(combine, plane_of(jnp.float32), 1 << 23, 1 << 19)(
        table, own, far, outer, inner
    ).reshape(LINES, CH, DEPTH)
    point_values, field, upstream = run(
        point_map,
        [stack_of(jnp.float32), stack_of(jnp.bfloat16), stack_of(jnp.bfloat16)],
        1 << 26,
        7 << 20,
    )(point, field, upstream)
    other = across(coarse)

    own_mix = jnp.einsum("ky,ycz->kcz", ahead[:, :LINES], coarse, precision=HIGH)
    own_mix = own_mix.reshape(RING, LINES, CH, DEPTH)
    far_weights = ahead[:, LINES:].reshape(RING, LINES, LINES)
    partial = [
        own_mix[n] + jnp.einsum("ky,ycz->kcz", far_weights[n], other, precision=HIGH) for n in range(RING)
    ]
    row_mixed = partial[3]
    for n in range(RING - 1):
        row_mixed = row_mixed + along(partial[n], AHEAD[n])
    mixed = jnp.einsum("dc,kcz->kdz", channel_w, row_mixed, precision=HIGH)
    delta = jnp.matmul(mixed - coarse, SYNTHESISE, precision=HIGH)
    after = moved(delta, -1)

    response, base, here, up, part_point = run(
        activate,
        [
            stack_of(jnp.bfloat16),
            stack_of(jnp.float32),
            plane_of(jnp.float32),
            plane_of(jnp.float32),
            jax.ShapeDtypeStruct((CH, DEPTH), jnp.float32),
        ],
        1 << 28,
        5 << 20,
        [
            SENT[0],
            pltpu.VMEM((PLANES, ROWS, DEPTH), jnp.float32),
            pltpu.VMEM((ROWS, ROWS), jnp.float32),
            SENT[1],
        ],
        in_specs=[VMEM] * 6,
        out_specs=[HBM, VMEM, VMEM, VMEM, VMEM],
    )(turned, point_values, field, upstream, delta.reshape(-1, DEPTH), after.reshape(-1, DEPTH))

    below = moved(up, 1)
    g_mixed = jnp.matmul((here + below).reshape(LINES, CH, DEPTH), SYNTHESISE.T, precision=HIGH)
    part_channels = jnp.einsum("kdz,kcz->dc", g_mixed, row_mixed, precision=HIGH)
    g_chan = jnp.einsum("dc,kdz->kcz", channel_w, g_mixed, precision=HIGH)
    small = part_point + jnp.pad(part_channels, ((0, 0), (0, DEPTH - CH)))
    packed = jnp.concatenate([g_chan.reshape(256, 128), small], 0)
    pieces = [packed] + [along(packed, -d) for d in BEHIND[1:]]
    planes = [piece[:256].reshape(16, 16, 128) for piece in pieces]

    weights = behind.reshape(RING, LINES, 2 * LINES)

    def lines_of(n, columns):
        return jnp.einsum("ky,kcz->ycz", weights[n][:, columns], planes[n], precision=HIGH)

    last = lines_of(RING - 1, slice(0, 2 * LINES))
    for_us = last[:LINES] + sum(lines_of(n, slice(0, LINES)) for n in range(RING - 1))
    for_them = last[LINES:] + sum(lines_of(n, slice(LINES, 2 * LINES)) for n in range(RING - 1))
    far = across(for_them)
    products = run(
        row_products,
        jax.ShapeDtypeStruct((PLANES, 24, 128), jnp.float32),
        1 << 25,
        1 << 20,
        in_specs=[VMEM, VMEM, ANY] + [VMEM] * RING,
    )(coarse.reshape(256, 128), other.reshape(256, 128), for_them, *pieces)
    products = run(add_up, jax.ShapeDtypeStruct((24, 128), jnp.float32), 1 << 16, 1 << 18)(
        lax.all_to_all(products, "gx", 0, 0)
    )
    their_products = across(products)
    g_coarse = for_us + far
    spread = jnp.matmul(g_coarse - g_mixed, ANALYSE.T, precision=HIGH).reshape(256, 128)
    far = routed(spread, -2, -2)
    outer = routed(spread, -1, 1)
    around = [far, outer, routed(spread, 1, -1), spread]
    at = lax.broadcasted_iota(jnp.int32, (128, 128), 0)
    turn = jnp.asarray(np.repeat(np.array(BEHIND * 2), 16))[:, None]
    k_side = jnp.where(at < 64, side, 1 - side)
    k_at = (k_side * RING + lax.rem(spot + turn + RING, RING)) * LINES + lax.rem(at, LINES)
    placed = (k_at == lax.broadcasted_iota(jnp.int32, (128, 128), 1)).astype(jnp.float32)
    grad_pressure = run(
        spread_out,
        stack_of(jnp.bfloat16),
        1 << 22,
        4 << 20,
        SENT,
        in_specs=[VMEM] * 5,
        out_specs=HBM,
    )(base, *around)
    grad_rows, grad_channels, grad_point = run(
        finish,
        [jax.ShapeDtypeStruct(shape, jnp.float32) for shape in ((16, 128), (16, 16), (16, 16))],
        1 << 18,
        1 << 18,
    )(products, their_products, placed)
    return (
        response.reshape(pressure.shape),
        grad_pressure.reshape(pressure.shape),
        grad_rows.T,
        grad_channels,
        grad_point,
    )


def solution(mesh):
    return jax.shard_map(
        shards,
        mesh=mesh,
        in_specs=(P("gx", "gy", None, None), P("gx", "gy", None, None), P(), P(), P()),
        out_specs=(P("gx", "gy", None, None), P("gx", "gy", None, None), P(None, "gy"), P(), P()),
        check_vma=False,
    )
```

```python
import jax
import jax.numpy as jnp
import numpy as np
from jax import lax
from jax.experimental import pallas as pl
from jax.experimental.pallas import tpu as pltpu
from jax.sharding import PartitionSpec as P

DEPTH = 128
LEVELS = 4
PLANES = 16
LINES = 16
CH = 16
N_GY = 8
RING = 4
AHEAD = (2, 1, 3, 0)
BEHIND = (0, -2, -1, -3)
ROWS = 64
LIMIT = 12
GELU_A = float(np.sqrt(2.0 / np.pi))
GELU_B = 0.044715 * GELU_A
SHIFTS = (-1, 0, 1, 2)

HIGH = lax.Precision.HIGHEST


def lift_rows(rows):
    even, odd = rows[:, 0::2], rows[:, 1::2]
    detail = odd - 0.5 * (even + np.roll(even, -1, 1))
    smooth = even + 0.25 * (np.roll(detail, 1, 1) + detail)
    return smooth, detail


def depth_table():
    table = np.eye(DEPTH)
    for level in range(LEVELS):
        width = DEPTH >> level
        smooth, detail = lift_rows(table[:, :width])
        table = np.concatenate([smooth, detail, table[:, width:]], 1)
    return table


def depth_back():
    table = np.eye(DEPTH)
    for level in reversed(range(LEVELS)):
        width = DEPTH >> level
        smooth, detail = table[:, : width // 2], table[:, width // 2 : width]
        even = smooth - 0.25 * (np.roll(detail, 1, 1) + detail)
        odd = detail + 0.5 * (even + np.roll(even, -1, 1))
        head = np.stack([even, odd], 2).reshape(DEPTH, width)
        table = np.concatenate([head, table[:, width:]], 1)
    return table


def plane_weights():
    total = 8 * PLANES
    table = np.eye(total)
    for level in range(LEVELS):
        table = lift_rows(table)[0]
    own = table[3 * PLANES : 4 * PLANES]
    return np.stack([own[:, 3 + shift] for shift in SHIFTS])


ANALYSE = depth_table().astype(np.float32)
SYNTHESISE = depth_back().astype(np.float32)
WEIGHTS = plane_weights().astype(np.float32)
RISE = (np.arange(PLANES) / PLANES).astype(np.float32)


def moved(block, distance):
    size = lax.axis_size("gx")
    return lax.ppermute(block, "gx", [(i, (i + distance) % size) for i in range(size)])


def routed(block, *hops):
    size = lax.axis_size("gx")
    route = [(i, (i + hops[i % 2]) % size) for i in range(size)]
    return lax.ppermute(block, "gx", route)


def across(block):
    return lax.ppermute(block, "gy", [(i, (i + RING) % N_GY) for i in range(N_GY)])


def along(block, distance):
    route = [(i, i // RING * RING + (i + distance) % RING) for i in range(N_GY)]
    return lax.ppermute(block, "gy", route)


def plane_sums(field_ref, own_ref, inner_ref, outer_ref, far_ref):
    odd = lax.rem(lax.axis_index("gx"), 2) == 1
    for first in range(0, LINES * CH, 32):
        rows = pl.ds(first, 32)
        sums = [None] * 4
        for j in range(PLANES):
            plane = field_ref[j, rows, :].astype(jnp.float32)
            for k in range(4):
                if WEIGHTS[k, j] != 0.0:
                    term = plane * float(WEIGHTS[k, j])
                    sums[k] = term if sums[k] is None else sums[k] + term
        own_ref[rows, :] = sums[1]
        inner_ref[rows, :] = jnp.where(odd, sums[0], sums[2])
        outer_ref[rows, :] = jnp.where(odd, sums[2], sums[0])
        far_ref[rows, :] = sums[3]


def prepare(table_ref, point_ref, rows_ref, after_ref, kept_ref, map_ref, turned_ref, ahead_ref, behind_ref):
    kept_ref[...] = table_ref[...]
    at_row = lax.broadcasted_iota(jnp.int32, (ROWS, CH), 0)
    at_column = lax.broadcasted_iota(jnp.int32, (ROWS, CH), 1)
    tall = (lax.rem(at_row, CH) == at_column).astype(jnp.bfloat16)
    at_row = lax.broadcasted_iota(jnp.int32, (ROWS, ROWS), 0)
    at_column = lax.broadcasted_iota(jnp.int32, (ROWS, ROWS), 1)
    same = at_row // CH == at_column // CH
    point = point_ref[...]
    for turn, dims in enumerate(((1, 0), (1, 1))):
        mapped = lax.dot_general(
            tall, point, (((dims[0],), (dims[1],)), ((), ())), preferred_element_type=jnp.float32
        )
        mapped = lax.dot_general(
            mapped.astype(jnp.bfloat16), tall, (((1,), (1,)), ((), ())), preferred_element_type=jnp.float32
        )
        mapped = jnp.where(same, mapped, 0.0).astype(jnp.bfloat16)
        if turn:
            turned_ref[...] = jnp.concatenate([mapped, mapped], 1)
        else:
            map_ref[...] = mapped

    me = lax.axis_index("gy")
    side, spot = me // RING, lax.rem(me, RING)

    def chosen(count, first_side, steps):
        row = lax.broadcasted_iota(jnp.int32, (count, 128), 0)
        column = lax.broadcasted_iota(jnp.int32, (count, 128), 1)
        step = jnp.zeros_like(row)
        for n, distance in enumerate(steps):
            step = jnp.where(row // LINES == n, distance, step)
        at = (first_side * RING + lax.rem(spot + step + RING, RING)) * LINES + lax.rem(row, LINES)
        return (at == column).astype(jnp.bfloat16)

    lines = jnp.concatenate([chosen(LINES, side, (0,)), chosen(LINES, 1 - side, (0,))], 0)
    for ref, steps in ((ahead_ref, AHEAD), (behind_ref, BEHIND)):
        taken = jnp.dot(chosen(RING * LINES, side, steps), rows_ref[...], preferred_element_type=jnp.float32)
        ref[...] = lax.dot_general(
            taken.astype(jnp.bfloat16), lines, (((1,), (1,)), ((), ())), preferred_element_type=jnp.float32
        )


def combine(table_ref, *refs):
    total = sum(ref[...] for ref in refs[:-1])
    refs[-1][...] = jnp.dot(total, table_ref[...], precision=HIGH, preferred_element_type=jnp.float32)


def point_map(point_ref, field_ref, cotangent_ref, out_ref, field_kept_ref, cotangent_kept_ref):
    point = point_ref[...]

    @pl.loop(0, STEPS)
    def _(step):
        rows = pl.ds(pl.multiple_of(step * ROWS, ROWS), ROWS)
        for j in range(0, PLANES, 2):
            pair = jnp.concatenate([field_ref[j, rows, :], field_ref[j + 1, rows, :]], 1)
            mapped = jnp.dot(point, pair, preferred_element_type=jnp.float32) + pair.astype(jnp.float32)
            for n in range(2):
                out_ref[j + n, rows, :] = mapped[:, n * DEPTH : n * DEPTH + DEPTH]
                field_kept_ref[j + n, rows, :] = field_ref[j + n, rows, :]
                cotangent_kept_ref[j + n, rows, :] = cotangent_ref[j + n, rows, :]


def activate(
    turned_ref, mapped_ref, field_ref, cotangent_ref, delta_ref, after_ref,
    response_ref, base_ref, here_ref, up_ref, grad_ref, kept_ref, g_ref, acc_ref, sems,
):
    def chunk(step):
        rows = pl.ds(step * ROWS, ROWS)
        return pltpu.make_async_copy(kept_ref.at[:, rows, :], response_ref.at[:, rows, :], sems.at[step])

    turned = turned_ref[...]
    acc_ref[...] = jnp.zeros_like(acc_ref)
    for step in range(STEPS):
        for first in range(0, ROWS, 32):
            rows = pl.ds(step * ROWS + first, 32)
            delta = delta_ref[rows, :]
            slope = (after_ref[rows, :] - delta) * (1.0 / PLANES)
            base = delta + slope * float(PLANES)
            total = jnp.zeros_like(delta)
            up = jnp.zeros_like(delta)
            for at in range(PLANES - 1, -1, -1):
                base = base - slope
                value = mapped_ref[at, rows, :] + base
                square = value * value
                half = 0.5 + 0.5 * jnp.tanh(value * (GELU_A + GELU_B * square))
                active = value * half
                kept_ref[at, rows, :] = active.astype(jnp.bfloat16)
                rate = half + (active * (1.0 - half)) * (2.0 * GELU_A + 6.0 * GELU_B * square)
                g_pre = rate * cotangent_ref[at, rows, :].astype(jnp.float32)
                g_ref[at, pl.ds(first, 32), :] = g_pre
                total = total + g_pre
                if at:
                    up = up + total
            up = up * (1.0 / PLANES)
            here_ref[rows, :] = total - up
            up_ref[rows, :] = up
        chunk(step).start()
        rows = pl.ds(step * ROWS, ROWS)
        acc = acc_ref[...]
        for j in range(PLANES):
            g_pre = g_ref[j]
            high = g_pre.astype(jnp.bfloat16)
            low = (g_pre - high.astype(jnp.float32)).astype(jnp.bfloat16)
            base_ref[j, rows, :] = g_pre + jnp.dot(
                turned, jnp.concatenate([high, low], 0), preferred_element_type=jnp.float32
            )
            plane = field_ref[j, rows, :]
            acc = acc + lax.dot_general(
                jnp.concatenate([high, low], 1),
                jnp.concatenate([plane, plane], 1),
                (((1,), (1,)), ((), ())),
                preferred_element_type=jnp.float32,
            )
        acc_ref[...] = acc

    row = lax.broadcasted_iota(jnp.int32, (ROWS, ROWS), 0)
    column = lax.broadcasted_iota(jnp.int32, (ROWS, ROWS), 1)
    kept = jnp.where(row // CH == column // CH, acc_ref[...], 0.0)
    folded = kept[0:CH]
    for n in range(1, ROWS // CH):
        folded = folded + kept[n * CH : n * CH + CH]
    source = lax.broadcasted_iota(jnp.int32, (ROWS, DEPTH), 0)
    target = lax.broadcasted_iota(jnp.int32, (ROWS, DEPTH), 1)
    fold = (lax.rem(source, CH) + CH == target).astype(jnp.float32)
    grad_ref[...] = jnp.dot(folded, fold, precision=HIGH, preferred_element_type=jnp.float32)
    for step in range(STEPS):
        chunk(step).wait()


def halves(values):
    high = values.astype(jnp.bfloat16)
    return high, (values - high.astype(jnp.float32)).astype(jnp.bfloat16)


def row_products(own_ref, other_ref, after_ref, also_ref, *refs):
    out_ref, pieces = refs[-1], refs[:-1]
    total = jnp.zeros((2 * LINES, RING * LINES), jnp.float32)
    for c in range(CH):
        lines = pl.ds(c, LINES, stride=CH)
        left, left_low = halves(jnp.concatenate([own_ref[lines, :], other_ref[lines, :]], 0))
        right, right_low = halves(jnp.concatenate([ref[lines, :] for ref in pieces], 0))
        total = total + lax.dot_general(
            jnp.concatenate([left, left, left_low], 1),
            jnp.concatenate([right, right_low, right], 1),
            (((1,), (1,)), ((), ())),
            preferred_element_type=jnp.float32,
        )
    small = pl.ds(LINES * CH, CH)
    products = jnp.concatenate([total[:LINES], total[LINES:]], 1)
    sums = sum(ref[small, :] for ref in pieces)
    sums = jnp.concatenate([sums[4 * n : 4 * n + 4, 0:32] for n in range(4)], 1)
    for n in range(PLANES):
        out_ref[n, 0:LINES, :] = products
        out_ref[n, LINES : LINES + 4, :] = sums


def spread_out(base_ref, far_ref, outer_ref, inner_ref, own_ref, out_ref, kept_ref, sems):
    odd = lax.rem(lax.axis_index("gx"), 2) == 1

    def chunk(step):
        rows = pl.ds(step * ROWS, ROWS)
        return pltpu.make_async_copy(kept_ref.at[:, rows, :], out_ref.at[:, rows, :], sems.at[step])

    for step in range(STEPS):
        for first in range(step * ROWS, (step + 1) * ROWS, 32):
            rows = pl.ds(first, 32)
            inner, outer = inner_ref[rows, :], outer_ref[rows, :]
            around = [
                jnp.where(odd, inner, outer),
                own_ref[rows, :],
                jnp.where(odd, outer, inner),
                far_ref[rows, :],
            ]
            for j in range(PLANES):
                total = base_ref[j, rows, :]
                for k in range(4):
                    if WEIGHTS[k, j] != 0.0:
                        total = total + around[k] * float(WEIGHTS[k, j])
                kept_ref[j, rows, :] = total.astype(jnp.bfloat16)
        chunk(step).start()
    for step in range(STEPS):
        chunk(step).wait()


STEPS = LINES * CH // ROWS


def plane_of(kind):
    return jax.ShapeDtypeStruct((LINES * CH, DEPTH), kind)


def stack_of(kind):
    return jax.ShapeDtypeStruct((PLANES, LINES * CH, DEPTH), kind)


def add_up(parts_ref, out_ref):
    total = parts_ref[0]
    for n in range(1, PLANES):
        total = total + parts_ref[n]
    out_ref[...] = total


def finish(own_ref, their_ref, placed_ref, rows_ref, channels_ref, point_ref):
    joined = jnp.concatenate([own_ref[0:LINES, 0:64], their_ref[0:LINES, 64:128]], 1)
    rows_ref[...] = jnp.dot(joined, placed_ref[...], precision=HIGH, preferred_element_type=jnp.float32)
    small = own_ref[LINES : LINES + 4, :] + their_ref[LINES : LINES + 4, :]
    for n in range(4):
        channels_ref[4 * n : 4 * n + 4, :] = small[:, 32 * n : 32 * n + CH]
        point_ref[4 * n : 4 * n + 4, :] = small[:, 32 * n + CH : 32 * n + 2 * CH]


VMEM = pl.BlockSpec()
HBM = pl.BlockSpec(memory_space=pltpu.HBM)
ANY = pl.BlockSpec(memory_space=pl.ANY)
SENT = [pltpu.VMEM((PLANES, LINES * CH, DEPTH), jnp.bfloat16), pltpu.SemaphoreType.DMA((STEPS,))]


def run(kernel, out_shape, flops, size, scratch=(), **where):
    return pl.pallas_call(
        kernel,
        out_shape=out_shape,
        scratch_shapes=scratch,
        cost_estimate=pl.CostEstimate(flops=flops, bytes_accessed=size, transcendentals=0),
        compiler_params=pltpu.CompilerParams(vmem_limit_bytes=LIMIT * 1024 * 1024),
        **where,
    )


def shards(pressure, cotangent, mix_rows, mix_channels, pointwise):
    me = lax.axis_index("gy")
    side, spot = me // RING, lax.rem(me, RING)
    channel_w = mix_channels.astype(jnp.float32)
    field = pressure.reshape(PLANES, LINES * CH, DEPTH)
    upstream = cotangent.reshape(PLANES, LINES * CH, DEPTH)

    own, inner, outer, far = run(plane_sums, [plane_of(jnp.float32)] * 4, 1 << 22, 3 << 19)(field)
    table, point, turned, ahead, behind = run(
        prepare,
        [
            jax.ShapeDtypeStruct((DEPTH, DEPTH), jnp.float32),
            jax.ShapeDtypeStruct((ROWS, ROWS), jnp.bfloat16),
            jax.ShapeDtypeStruct((ROWS, 2 * ROWS), jnp.bfloat16),
            jax.ShapeDtypeStruct((RING * LINES, 2 * LINES), jnp.float32),
            jax.ShapeDtypeStruct((RING * LINES, 2 * LINES), jnp.float32),
        ],
        1 << 20,
        1 << 18,
        in_specs=[VMEM, VMEM, VMEM, ANY],
    )(jnp.asarray(ANALYSE), pointwise, mix_rows, own)
    far = routed(far, 2, 2)
    outer = routed(outer, -1, 1)
    inner = routed(inner, 1, -1)
    coarse = run(combine, plane_of(jnp.float32), 1 << 23, 1 << 19)(
        table, own, far, outer, inner
    ).reshape(LINES, CH, DEPTH)
    point_values, field, upstream = run(
        point_map,
        [stack_of(jnp.float32), stack_of(jnp.bfloat16), stack_of(jnp.bfloat16)],
        1 << 26,
        7 << 20,
    )(point, field, upstream)
    other = across(coarse)

    own_mix = jnp.einsum("ky,ycz->kcz", ahead[:, :LINES], coarse, precision=HIGH)
    own_mix = own_mix.reshape(RING, LINES, CH, DEPTH)
    far_weights = ahead[:, LINES:].reshape(RING, LINES, LINES)
    partial = [
        own_mix[n] + jnp.einsum("ky,ycz->kcz", far_weights[n], other, precision=HIGH) for n in range(RING)
    ]
    row_mixed = partial[3]
    for n in range(RING - 1):
        row_mixed = row_mixed + along(partial[n], AHEAD[n])
    mixed = jnp.einsum("dc,kcz->kdz", channel_w, row_mixed, precision=HIGH)
    delta = jnp.matmul(mixed - coarse, SYNTHESISE, precision=HIGH)
    after = moved(delta, -1)

    response, base, here, up, part_point = run(
        activate,
        [
            stack_of(jnp.bfloat16),
            stack_of(jnp.float32),
            plane_of(jnp.float32),
            plane_of(jnp.float32),
            jax.ShapeDtypeStruct((CH, DEPTH), jnp.float32),
        ],
        1 << 28,
        5 << 20,
        [
            SENT[0],
            pltpu.VMEM((PLANES, ROWS, DEPTH), jnp.float32),
            pltpu.VMEM((ROWS, ROWS), jnp.float32),
            SENT[1],
        ],
        in_specs=[VMEM] * 6,
        out_specs=[HBM, VMEM, VMEM, VMEM, VMEM],
    )(turned, point_values, field, upstream, delta.reshape(-1, DEPTH), after.reshape(-1, DEPTH))

    below = moved(up, 1)
    g_mixed = jnp.matmul((here + below).reshape(LINES, CH, DEPTH), SYNTHESISE.T, precision=HIGH)
    part_channels = jnp.einsum("kdz,kcz->dc", g_mixed, row_mixed, precision=HIGH)
    g_chan = jnp.einsum("dc,kdz->kcz", channel_w, g_mixed, precision=HIGH)
    small = part_point + jnp.pad(part_channels, ((0, 0), (0, DEPTH - CH)))
    packed = jnp.concatenate([g_chan.reshape(256, 128), small], 0)
    pieces = [packed] + [along(packed, -d) for d in BEHIND[1:]]
    planes = [piece[:256].reshape(16, 16, 128) for piece in pieces]

    weights = behind.reshape(RING, LINES, 2 * LINES)

    def lines_of(n, columns):
        return jnp.einsum("ky,kcz->ycz", weights[n][:, columns], planes[n], precision=HIGH)

    last = lines_of(RING - 1, slice(0, 2 * LINES))
    for_us = last[:LINES] + sum(lines_of(n, slice(0, LINES)) for n in range(RING - 1))
    for_them = last[LINES:] + sum(lines_of(n, slice(LINES, 2 * LINES)) for n in range(RING - 1))
    far = across(for_them)
    products = run(
        row_products,
        jax.ShapeDtypeStruct((PLANES, 24, 128), jnp.float32),
        1 << 25,
        1 << 20,
        in_specs=[VMEM, VMEM, ANY, ANY] + [VMEM] * RING,
    )(coarse.reshape(256, 128), other.reshape(256, 128), for_them, for_us, *pieces)
    products = run(add_up, jax.ShapeDtypeStruct((24, 128), jnp.float32), 1 << 16, 1 << 18)(
        lax.all_to_all(products, "gx", 0, 0)
    )
    their_products = across(products)
    g_coarse = for_us + far
    spread = jnp.matmul(g_coarse - g_mixed, ANALYSE.T, precision=HIGH).reshape(256, 128)
    far = routed(spread, -2, -2)
    outer = routed(spread, -1, 1)
    around = [far, outer, routed(spread, 1, -1), spread]
    at = lax.broadcasted_iota(jnp.int32, (128, 128), 0)
    turn = jnp.asarray(np.repeat(np.array(BEHIND * 2), 16))[:, None]
    k_side = jnp.where(at < 64, side, 1 - side)
    k_at = (k_side * RING + lax.rem(spot + turn + RING, RING)) * LINES + lax.rem(at, LINES)
    placed = (k_at == lax.broadcasted_iota(jnp.int32, (128, 128), 1)).astype(jnp.float32)
    grad_pressure = run(
        spread_out,
        stack_of(jnp.bfloat16),
        1 << 22,
        4 << 20,
        SENT,
        in_specs=[VMEM] * 5,
        out_specs=HBM,
    )(base, *around)
    grad_rows, grad_channels, grad_point = run(
        finish,
        [jax.ShapeDtypeStruct(shape, jnp.float32) for shape in ((16, 128), (16, 16), (16, 16))],
        1 << 18,
        1 << 18,
    )(products, their_products, placed)
    return (
        response.reshape(pressure.shape),
        grad_pressure.reshape(pressure.shape),
        grad_rows.T,
        grad_channels,
        grad_point,
    )


def solution(mesh):
    return jax.shard_map(
        shards,
        mesh=mesh,
        in_specs=(P("gx", "gy", None, None), P("gx", "gy", None, None), P(), P(), P()),
        out_specs=(P("gx", "gy", None, None), P("gx", "gy", None, None), P(None, "gy"), P(), P()),
        check_vma=False,
    )
```
